256 devices in a mesh: dp: 32 (over y, z_lo, core), tensor: 8 (over x, z_hi).
Axes of the slice: x: 4, y: 4, z: 8 (z_hi: 2, z_lo: 4; z = z_hi * 4 + z_lo), core: 2. Of those that a mesh axis runs over, the one named last changes fastest.
Arguments:
- gradient: bfloat16 [3200, 12800], P('dp', 'tensor'), may hold values from -200 to 200
Outputs:
- update: bfloat16 [3200, 12800], P('dp', 'tensor')
- residual: float32 [1600, 12800], P('dp', 'tensor')
The draws below stay inside these ranges and needn't reach their ends.
All inputs are finite; a program needn't handle non-finite values.
Results may differ from the reference program's by a relative error of at most 0.012.
Values may be sent and summed in bfloat16 or wider, within the bound.
A program may use at most 128 MiB of HBM per device.

```python
import math
import jax
import jax.numpy as jnp
from jax import lax

D = 3200
FF = 12800
BLK = 1600
N_DP = 32


def draw_gradient(key, part):
    key = jax.random.fold_in(key, 7)
    keys = jax.random.split(key, 3)
    row_pos = jnp.arange(D, dtype=jnp.float32) / D
    col_pos = jnp.arange(FF, dtype=jnp.float32)
    within = jnp.mod(col_pos, BLK) / BLK
    block_pos = jnp.floor(col_pos / BLK) / (FF // BLK)
    trend = jnp.sqrt(1.0 + 2.0 * row_pos)[:, None] * jnp.sqrt((1.0 + 2.0 * within) * (1.0 + 2.0 * block_pos))[None, :]
    spread = math.log(10.0)
    values = jnp.clip(jax.random.normal(keys[0], (D, FF), jnp.float32), -5.0, 5.0)
    row_scale = jnp.exp(jax.random.uniform(keys[1], (D, 1), jnp.float32, -0.5 * spread, 0.5 * spread))
    col_scale = jnp.exp(jax.random.uniform(keys[2], (1, FF), jnp.float32, -0.5 * spread, 0.5 * spread))
    return jnp.clip(values * row_scale * col_scale * trend, -200.0, 200.0).astype(jnp.bfloat16)


def setup_inputs(seed: int = 0) -> dict:
    streams_of = jax.random.split(jax.random.key(seed), 2)
    return {
        "gradient": draw_gradient(jax.random.fold_in(streams_of[1], 71), 0),
    }


HIGH = lax.Precision.HIGHEST
DAMP = 0.002
EPSILON = 1e-06

def block_gram(column_block):
    pieces = column_block.reshape(N_DP, D // N_DP, BLK)

    def add_piece(total, piece):
        term = jnp.dot(piece.T, piece, preferred_element_type=jnp.float32).astype(jnp.bfloat16)
        term = lax.optimization_barrier(term)
        return (total + term.astype(jnp.float32), None)
    total, _ = lax.scan(add_piece, jnp.zeros((BLK, BLK), jnp.float32), pieces)
    return total

def block_root(gram):
    identity = jnp.eye(BLK, dtype=jnp.float32)
    norm = jnp.sqrt(jnp.sum(gram * gram))
    scale = 0.25 * (norm + DAMP * norm)
    moment_first = (gram + DAMP * norm * identity) / scale
    root_start = identity * scale ** (-0.25)
    affine_first = (5.0 * identity - moment_first) * 0.25
    root_first = jnp.dot(affine_first, root_start, precision=HIGH)
    squared = jnp.dot(affine_first, affine_first, precision=HIGH)
    quartic = jnp.dot(squared, squared, precision=HIGH)
    moment_next = jnp.dot(quartic, moment_first, precision=HIGH)
    affine_next = (5.0 * identity - moment_next) * 0.25
    return (jnp.dot(affine_next, root_first, precision=HIGH), moment_next - identity)

def reference(gradient):
    block_count = FF // BLK
    column_blocks = gradient.reshape(D, block_count, BLK).transpose(1, 0, 2)

    def one_block(column_block):
        root, leftover = block_root(block_gram(column_block))
        root = root.astype(jnp.bfloat16)
        return (jnp.dot(column_block, root, preferred_element_type=jnp.float32), leftover)
    preconditioned, leftovers = lax.map(one_block, column_blocks)
    pre_total = jnp.sum(preconditioned * preconditioned)
    ratio = math.sqrt(D * FF) / jnp.sqrt(pre_total + EPSILON)
    update = (preconditioned * ratio).astype(jnp.bfloat16)
    residual = leftovers.transpose(1, 0, 2).reshape(BLK, FF)
    return (update.transpose(1, 0, 2).reshape(D, FF), residual)
```

```python
import functools
import math

import jax
import jax.numpy as jnp
from jax import lax
from jax.experimental import pallas as pl
from jax.experimental.pallas import tpu as pltpu
from jax.sharding import PartitionSpec as P

D = 3200
FF = 12800
BLK = 1600
DAMP = 0.002
EPSILON = 1e-06

T = 128
NB = 13
W = NB * T
HALF = 7
KD = 112
ROWS = 100
OWN = 50
XG = 104
XR = 160
NY, NZ, NC = 4, 4, 2
CH = 3
BF = jnp.bfloat16
F32 = jnp.float32
STAGE = 9


def tile_bands(q):
    i = (q // HALF) % NB
    return i, (i + q % HALF) % NB


def kernel(
    n_dp,
    n_tensor,
    g_ref,
    upd_ref,
    res_ref,
    gall,
    acc,
    part,
    zrecv,
    tri,
    full,
    x,
    xb,
    t_ref,
    sq,
    red1,
    red2,
    g_send,
    g_recv,
    z_send,
    z_recv,
    t_send,
    t_recv,
    r1_send,
    r1_recv,
    r2_send,
    r2_recv,
):
    dp = lax.axis_index("dp")
    tensor = lax.axis_index("tensor")
    a, b, c = dp // (NZ * NC), (dp // NC) % NZ, dp % NC

    def at(a_, b_, c_):
        return ((a_ * NZ + b_) * NC + c_, tensor)

    up = at((a + 1) % NY, b, c)
    down = at((a + NY - 1) % NY, b, c)
    pair = at(a, b, 1 - c)

    barrier = pltpu.get_barrier_semaphore()
    for k in range(1, n_dp):
        pl.semaphore_signal(
            barrier, inc=1, device_id=((dp + k) % n_dp, tensor), device_id_type=pl.DeviceIdType.MESH
        )
    for k in range(1, n_tensor):
        pl.semaphore_signal(
            barrier, inc=1, device_id=(dp, (tensor + k) % n_tensor), device_id_type=pl.DeviceIdType.MESH
        )

    for i in range(NB):
        gall[i, 0:KD, :] = jnp.zeros((KD, T), BF)
        w = min(T, BLK - i * T)
        gall[i, 0:ROWS, 0:w] = g_ref[:, i * T : i * T + w]

    pl.semaphore_wait(barrier, n_dp - 1 + n_tensor - 1)

    def remote(src, dst, send, recv, to):
        return pltpu.make_async_remote_copy(
            src_ref=src,
            dst_ref=dst,
            send_sem=send,
            recv_sem=recv,
            device_id=to,
            device_id_type=pl.DeviceIdType.MESH,
        )

    LO, HI = pl.ds(0, 7), pl.ds(7, 6)
    parts = (LO, HI)

    def rows(ra, rc):
        return pl.ds((2 * ra + rc) * KD, KD)

    def g_index(ra, rc, h):
        return (2 * ra + rc) * 2 + h

    started = []

    def g_copy(h, src_slot, dst_slot, to):
        n = g_index(dst_slot[0], dst_slot[1], h)
        return remote(
            gall.at[parts[h], rows(*src_slot), :],
            gall.at[parts[h], rows(*dst_slot), :],
            g_send.at[n],
            g_recv.at[n],
            to,
        )

    def g_go(*args):
        copy = g_copy(*args)
        copy.start()
        started.append(copy)

    def g_wait(slot, h):
        g_copy(h, slot, slot, pair).wait_recv()

    def accumulate(ra, first):
        band_rows = pl.ds(2 * ra * KD, 2 * KD)

        def tile(e, carry):
            i, j = tile_bands(24 * a + 12 * c + e)
            value = lax.dot_general(
                gall[i, band_rows, :],
                gall[j, band_rows, :],
                (((0,), (0,)), ((), ())),
                preferred_element_type=F32,
            )
            acc[e] = value if first else acc[e] + value
            return carry

        lax.fori_loop(0, 12, tile, 0)

    own = (0, 0)
    g_go(0, own, (3, 0), up)
    g_go(1, own, (1, 0), down)
    g_go(1, own, (3, 0), up)
    g_go(0, own, (1, 0), down)
    g_go(0, own, (0, 1), pair)
    g_go(1, own, (0, 1), pair)
    g_wait((0, 1), 0)
    g_wait((0, 1), 1)
    accumulate(0, True)
    g_wait((3, 0), 0)
    g_go(0, (3, 0), (2, 0), up)
    g_go(0, (3, 0), (3, 1), pair)
    g_wait((1, 0), 1)
    g_go(1, (1, 0), (2, 0), down)
    g_go(1, (1, 0), (1, 1), pair)
    g_wait((3, 0), 1)
    g_go(1, (3, 0), (3, 1), pair)
    g_wait((1, 0), 0)
    g_go(0, (1, 0), (1, 1), pair)
    g_wait((3, 1), 0)
    g_wait((3, 1), 1)
    accumulate(3, False)
    g_wait((1, 1), 0)
    g_wait((1, 1), 1)
    accumulate(1, False)
    g_wait((2, 0), 0)
    g_go(0, (2, 0), (2, 1), pair)
    g_wait((2, 0), 1)
    g_go(1, (2, 0), (2, 1), pair)
    g_wait((2, 1), 0)
    g_wait((2, 1), 1)
    accumulate(2, False)

    def round_tile(e, carry):
        part[e] = acc[e].astype(BF)
        return carry

    lax.fori_loop(0, 12, round_tile, 0)

    def z_copy(k):
        bk = (b + k) % NZ
        return remote(
            part.at[pl.ds(CH * bk, CH)],
            zrecv.at[k - 1],
            z_send.at[k - 1],
            z_recv.at[k - 1],
            at(a, bk, c),
        )

    z_copies = [z_copy(k) for k in range(1, NZ)]
    for copy in z_copies:
        copy.start()
    for copy in z_copies:
        copy.wait_recv()

    def chunk(ra, rc, k):
        a_ = (a + ra) % NY
        c_ = c if rc == 0 else 1 - c
        b_ = (b + NZ - k) % NZ
        return 24 * a_ + 12 * c_ + CH * b_

    mine = chunk(0, 0, 0)

    def sum_tile(e, carry):
        total = acc[CH * b + e]
        for k in range(NZ - 1):
            total = total + zrecv[k, e].astype(F32)
        tri[mine + e] = total.astype(BF)
        return carry

    lax.fori_loop(0, CH, sum_tile, 0)

    def t_index(ra, rc, k):
        return (ra * NC + rc) * NZ + k

    def t_copy(held, label, to):
        place = pl.ds(chunk(*held), CH)
        n = t_index(*label)
        return remote(tri.at[place], tri.at[place], t_send.at[n], t_recv.at[n], to)

    def t_go(*args):
        copy = t_copy(*args)
        copy.start()
        started.append(copy)

    def t_wait(label):
        t_copy(label, label, pair).wait_recv()

    sq[...] = jnp.zeros_like(sq)

    def expand(label):
        first = chunk(*label)

        def tile(e, carry):
            q = first + e

            @pl.when(q < NB * HALF)
            def _():
                i, j = tile_bands(q)
                value = tri[q]
                wide = value.astype(F32)
                weight = jnp.where(q % HALF == 0, 1.0, 2.0)
                sq[...] += weight * jnp.sum((wide * wide).reshape(T // 8, 8, T), axis=0)
                ri = pl.ds(pl.multiple_of(i * T, T), T)
                rj = pl.ds(pl.multiple_of(j * T, T), T)
                full[rj, ri] = wide.T.astype(BF)
                full[ri, rj] = value

            return carry

        lax.fori_loop(0, CH, tile, 0)

    for k in range(1, NZ):
        t_go((0, 0, 0), (0, 0, k), at(a, (b + k) % NZ, c))
    for k in range(NZ):
        held = (0, 0, k)
        if k:
            t_wait(held)
        t_go(held, (3, 0, k), up)
        t_go(held, (1, 0, k), down)
        t_go(held, (0, 1, k), pair)
        expand(held)
    for k in range(NZ):
        held = (3, 0, k)
        t_wait(held)
        if k % 2 == 0:
            t_go(held, (2, 0, k), up)
        t_go(held, (3, 1, k), pair)
        held = (1, 0, k)
        t_wait(held)
        if k % 2 == 1:
            t_go(held, (2, 0, k), down)
        t_go(held, (1, 1, k), pair)
        expand((3, 0, k))
        expand((1, 0, k))
    for k in range(NZ):
        t_wait((0, 1, k))
        expand((0, 1, k))
    for k in range(NZ):
        held = (2, 0, k)
        t_wait(held)
        t_go(held, (2, 1, k), pair)
        expand(held)
    for k in range(NZ):
        t_wait((3, 1, k))
        expand((3, 1, k))
        t_wait((1, 1, k))
        expand((1, 1, k))
    for k in range(NZ):
        t_wait((2, 1, k))
        expand((2, 1, k))

    for copy in started + z_copies:
        copy.wait_send()

    norm = jnp.sqrt(jnp.sum(sq[...], keepdims=True))
    scale = 0.25 * (norm + DAMP * norm)
    inverse = 1.0 / scale
    damp = DAMP * norm * inverse
    root0 = lax.rsqrt(jnp.sqrt(scale))

    zero_rows = jnp.zeros((XG, T), F32)
    for i in range(NB):
        cols = slice(i * T, (i + 1) * T)
        x[0:XG, cols] = gall[i, 0:XG, :].astype(F32)
        xb[0, 0:XG, cols] = gall[i, 0:XG, :]
        row_ids = lax.broadcasted_iota(jnp.int32, (XR - XG, T), 0)
        col_ids = lax.broadcasted_iota(jnp.int32, (XR - XG, T), 1) + i * T
        unit = ((col_ids == row_ids + OWN * dp) & (row_ids < OWN)).astype(F32)
        x[XG:XR, cols] = unit
        xb[0, XG:XR, cols] = unit.astype(BF)

    chunks = [(n, min(256, W - n)) for n in range(0, W, 256)]

    def moment(source, count, n, w):
        product = jnp.dot(xb[source, 0:count, :], full[:, n : n + w], preferred_element_type=F32)
        return product * inverse + damp * x[0:count, n : n + w]

    def step(source, target, first):
        for n, w in chunks:
            m = moment(source, XR, n, w)
            old = x[:, n : n + w]
            new_g = 1.25 * old[0:XG] - 0.25 * m[0:XG]
            if first:
                new_e = m[XG:XR]
                t_ref[:, n : n + w] = new_g
            else:
                new_e = 1.25 * old[XG:XR] - 0.25 * m[XG:XR]
            new = jnp.concatenate([new_g, new_e], axis=0)
            x[:, n : n + w] = new
            xb[target, :, n : n + w] = new.astype(BF)

    step(0, 1, True)

    def middle(s, carry):
        step((s + 1) % 2, s % 2, False)
        return carry

    lax.fori_loop(0, 4, middle, 0)

    total = jnp.zeros((1, 1), F32)
    for n, w in chunks:
        m = moment(1, XG, n, w)
        p = (1.25 * t_ref[:, n : n + w] - 0.25 * m) * root0
        t_ref[:, n : n + w] = p
        total = total + jnp.sum(p * p, keepdims=True)

    red1[0] = jnp.broadcast_to(total, (1, T))
    copies = []
    for k in range(1, n_dp):
        copies.append(
            remote(
                red1.at[0], red1.at[k], r1_send.at[k], r1_recv.at[k], ((dp + k) % n_dp, tensor)
            )
        )
    for copy in copies:
        copy.start()

    for n, w in chunks:
        w = min(w, BLK - n)
        row_ids = lax.broadcasted_iota(jnp.int32, (OWN, w), 0) + OWN * dp
        col_ids = lax.broadcasted_iota(jnp.int32, (OWN, w), 1) + n
        unit = (row_ids == col_ids).astype(F32)
        res_ref[:, n : n + w] = x[XG : XG + OWN, n : n + w] - unit

    for copy in copies:
        copy.wait()
    red2[0] = jnp.sum(red1[...], axis=0)
    copies = []
    for k in range(1, n_tensor):
        copies.append(
            remote(
                red2.at[0],
                red2.at[k],
                r2_send.at[k],
                r2_recv.at[k],
                (dp, (tensor + k) % n_tensor),
            )
        )
    for copy in copies:
        copy.start()
    for copy in copies:
        copy.wait()
    layer = jnp.sum(red2[...], axis=0)[:, 0:1]
    ratio = math.sqrt(D * FF) / jnp.sqrt(layer + EPSILON)
    for n, w in chunks:
        w = min(w, BLK - n)
        upd_ref[:, n : n + w] = (t_ref[0:ROWS, n : n + w] * ratio).astype(BF)


def body(n_dp, n_tensor, gradient):
    dma = pltpu.SemaphoreType.DMA
    return pl.pallas_call(
        functools.partial(kernel, n_dp, n_tensor),
        out_shape=(
            jax.ShapeDtypeStruct((ROWS, BLK), BF),
            jax.ShapeDtypeStruct((OWN, BLK), F32),
        ),
        in_specs=[pl.BlockSpec(memory_space=pltpu.VMEM)],
        out_specs=(pl.BlockSpec(memory_space=pltpu.VMEM), pl.BlockSpec(memory_space=pltpu.VMEM)),
        scratch_shapes=[
            pltpu.VMEM((NB, 8 * KD, T), BF),
            pltpu.VMEM((12, T, T), F32),
            pltpu.VMEM((12, T, T), BF),
            pltpu.VMEM((NZ - 1, CH, T, T), BF),
            pltpu.VMEM((96, T, T), BF),
            pltpu.VMEM((W, W), BF),
            pltpu.VMEM((XR, W), F32),
            pltpu.VMEM((2, XR, W), BF),
            pltpu.VMEM((XG, W), F32),
            pltpu.VMEM((8, T), F32),
            pltpu.VMEM((n_dp, 1, T), F32),
            pltpu.VMEM((n_tensor, 1, T), F32),
            dma((16,)),
            dma((16,)),
            dma((NZ - 1,)),
            dma((NZ - 1,)),
            dma((32,)),
            dma((32,)),
            dma((n_dp,)),
            dma((n_dp,)),
            dma((n_tensor,)),
            dma((n_tensor,)),
        ],
        compiler_params=pltpu.CompilerParams(
            collective_id=0, has_side_effects=True, vmem_limit_bytes=48 * 1024 * 1024
        ),
        cost_estimate=pl.CostEstimate(flops=6_000_000_000, bytes_accessed=1_000_000, transcendentals=0),
    )(gradient)


def solution(mesh):
    return jax.shard_map(
        functools.partial(body, mesh.shape["dp"], mesh.shape["tensor"]),
        mesh=mesh,
        in_specs=(P("dp", "tensor"),),
        out_specs=(P("dp", "tensor"), P("dp", "tensor")),
        check_vma=False,
    )
```

```python
import functools
import math

import jax
import jax.numpy as jnp
from jax import lax
from jax.experimental import pallas as pl
from jax.experimental.pallas import tpu as pltpu
from jax.sharding import PartitionSpec as P

D = 3200
FF = 12800
BLK = 1600
DAMP = 0.002
EPSILON = 1e-06

T = 128
NB = 13
W = NB * T
HALF = 7
NEED = 10
EXT = 20
KD = 112
ROWS = 100
OWN = 50
XG = 104
XR = 160
NY, NZ, NC = 4, 4, 2
CH = 3
BF = jnp.bfloat16
F32 = jnp.float32
MESH = pl.DeviceIdType.MESH


def band_of(q):
    return q // HALF


def kernel(
    n_dp,
    n_tensor,
    g_hbm,
    upd_ref,
    res_ref,
    g_ref,
    gx,
    gall,
    acc,
    part,
    zrecv,
    tri,
    full,
    x,
    xb,
    t_ref,
    sq,
    red1,
    red2,
    in_sem,
    g_send,
    g_recv,
    z_send,
    z_recv,
    t_send,
    t_recv,
    r_send,
    r_recv,
):
    dp = lax.axis_index("dp")
    tensor = lax.axis_index("tensor")
    a, b, c = dp // (NZ * NC), (dp // NC) % NZ, dp % NC

    def at(a_, b_, c_):
        return ((a_ * NZ + b_) * NC + c_, tensor)

    a_up, a_down = (a + 1) % NY, (a + NY - 1) % NY
    up = at(a_up, b, c)
    down = at(a_down, b, c)
    pair = at(a, b, 1 - c)
    zs = (b, b + 1 - 2 * (b % 2), (b + 2) % NZ, NZ - 1 - b)

    barrier = pltpu.get_barrier_semaphore()
    greeted = [up, down, pair] + [at(a, zs[k], c) for k in range(1, NZ)]
    greeted += [(dp, (tensor + k) % n_tensor) for k in range(1, n_tensor)]
    for to in greeted:
        pl.semaphore_signal(barrier, inc=1, device_id=to, device_id_type=MESH)

    load = pltpu.make_async_copy(g_hbm, g_ref, in_sem)
    load.start()

    def lanes(first, count):
        return pl.ds(pl.multiple_of(first * T, T), count * T)

    def rows(ra, rc):
        return pl.ds((2 * ra + rc) * KD, KD)

    tail = slice(ROWS - ROWS % 16, KD)
    gx[tail, :] = jnp.zeros((KD - tail.start, EXT * T), BF)
    gx[:, BLK - BLK % T : W] = jnp.zeros((KD, T), BF)
    gall[:, NEED * T :] = jnp.zeros((8 * KD, T), BF)
    sq[...] = jnp.zeros_like(sq)
    load.wait()
    gx[0:ROWS, 0:BLK] = g_ref[...]
    gx[0:ROWS, W:] = g_ref[:, 0 : EXT * T - W]

    first_band = [band_of(24 * v) for v in (a, a_up, a_down)]
    gall[0:KD, 0 : NEED * T] = gx[:, lanes(first_band[0], NEED)]
    d_up = (first_band[1] + NB - first_band[0]) % NB
    d_down = (first_band[0] + NB - first_band[2]) % NB

    pl.semaphore_wait(barrier, len(greeted))

    def remote(src, dst, send, recv, to):
        return pltpu.make_async_remote_copy(
            src_ref=src, dst_ref=dst, send_sem=send, recv_sem=recv, device_id=to, device_id_type=MESH
        )

    started = []

    labels = [
        (3, 0, 3, 6),
        (1, 0, 1, 6),
        (3, 0, 0, 3),
        (3, 0, 9, 1),
        (1, 0, 0, 1),
        (1, 0, 7, 3),
        (2, 0, 0, 5),
        (2, 0, 5, 5),
        (0, 1, 0, NEED),
        (3, 1, 0, NEED),
        (1, 1, 0, NEED),
        (2, 1, 0, 5),
        (2, 1, 5, 5),
    ]

    def g_copy(n, src, to):
        ra, rc, first, count = labels[n]
        dst = gall.at[rows(ra, rc), pl.ds(first * T, count * T)]
        return remote(dst if src is None else src, dst, g_send.at[n], g_recv.at[n], to)

    def g_go(n, src, to):
        copy = g_copy(n, src, to)
        copy.start()
        started.append(copy)

    def g_own(n, base, to):
        g_go(n, gx.at[:, lanes(base + labels[n][2], labels[n][3])], to)

    def g_held(n, slot, first, to):
        g_go(n, gall.at[rows(*slot), lanes(first, labels[n][3])], to)

    def g_wait(n):
        g_copy(n, None, pair).wait_recv()

    q0 = 24 * a + 12 * c
    row0 = band_of(q0)
    local0 = row0 - first_band[0]

    def accumulate(start, count, first):
        for m in range(3):
            band = local0 + m
            value = lax.dot_general(
                gall[pl.ds(start, count), lanes(band, 1)],
                gall[pl.ds(start, count), lanes(band, HALF)],
                (((0,), (0,)), ((), ())),
                preferred_element_type=F32,
            )
            acc[m] = value if first else acc[m] + value

    g_own(0, first_band[1], up)
    g_own(1, first_band[2], down)
    g_held(8, (0, 0), 0, pair)
    g_own(2, first_band[1], up)
    g_own(4, first_band[2], down)
    g_own(3, first_band[1], up)
    g_own(5, first_band[2], down)
    g_wait(8)
    accumulate(0, 2 * KD, True)
    g_wait(0)
    g_held(6, (3, 0), d_up, up)
    g_wait(1)
    g_held(7, (1, 0), 5 - d_down, down)
    g_wait(2)
    g_wait(3)
    g_held(9, (3, 0), 0, pair)
    g_wait(4)
    g_wait(5)
    g_held(10, (1, 0), 0, pair)
    g_wait(9)
    accumulate(6 * KD, 2 * KD, False)
    g_wait(10)
    accumulate(2 * KD, 2 * KD, False)
    g_wait(6)
    g_held(11, (2, 0), 0, pair)
    g_wait(7)
    g_held(12, (2, 0), 5, pair)
    accumulate(4 * KD, KD, False)
    g_wait(11)
    g_wait(12)
    accumulate(5 * KD, KD, False)

    def held_tile(e):
        q = q0 + e
        return acc[band_of(q) - row0, :, lanes(q % HALF, 1)]

    def round_tile(e, carry):
        part[e] = held_tile(e).astype(BF)
        return carry

    lax.fori_loop(0, 12, round_tile, 0)

    z_copies = [
        remote(
            part.at[pl.ds(CH * zs[k], CH)],
            zrecv.at[k - 1],
            z_send.at[k - 1],
            z_recv.at[k - 1],
            at(a, zs[k], c),
        )
        for k in range(1, NZ)
    ]
    for copy in z_copies:
        copy.start()
    for copy in z_copies:
        copy.wait_recv()

    def chunk(ra, rc, k):
        return 24 * ((a + ra) % NY) + 12 * (c if rc == 0 else 1 - c) + CH * zs[k]

    mine = chunk(0, 0, 0)

    def sum_tile(e, carry):
        total = held_tile(CH * b + e)
        for k in range(NZ - 1):
            total = total + zrecv[k, e].astype(F32)
        tri[mine + e] = total.astype(BF)
        return carry

    lax.fori_loop(0, CH, sum_tile, 0)

    ALL, LO, HI = pl.ds(0, T), pl.ds(0, T // 2), pl.ds(T // 2, T // 2)

    def t_make(held, label, to, piece):
        ra, rc, k = label
        place = tri.at[pl.ds(chunk(*held), CH), piece, :]
        n = ((ra * NC + rc) * NZ + k) * 2 + (1 if piece is HI else 0)
        return remote(place, place, t_send.at[n], t_recv.at[n], to)

    def t_go(held, label, to, piece=ALL):
        copy = t_make(held, label, to, piece)
        copy.start()
        started.append(copy)

    def t_wait(label, piece=ALL):
        t_make(label, label, pair, piece).wait_recv()

    def expand(label):
        first = chunk(*label)

        def tile(e, carry):
            q = first + e

            @pl.when(q < NB * HALF)
            def _():
                i = band_of(q)
                j = (i + q % HALF) % NB
                value = tri[q]
                wide = value.astype(F32)
                weight = jnp.where(q % HALF == 0, 1.0, 2.0)
                sq[...] += weight * jnp.sum((wide * wide).reshape(T // 8, 8, T), axis=0)
                full[lanes(j, 1), lanes(i, 1)] = wide.T.astype(BF)
                full[lanes(i, 1), lanes(j, 1)] = value

            return carry

        lax.fori_loop(0, CH, tile, 0)

    def spread(k):
        held = (0, 0, k)
        t_go(held, (3, 0, k), up)
        t_go(held, (1, 0, k), down)
        t_go(held, (0, 1, k), pair)
        expand(held)

    def relay(k):
        t_wait((3, 0, k))
        t_go((3, 0, k), (2, 0, k), up, LO)
        t_go((3, 0, k), (3, 1, k), pair)
        t_wait((1, 0, k))
        t_go((1, 0, k), (2, 0, k), down, HI)
        t_go((1, 0, k), (1, 1, k), pair)

    def relayed(k):
        t_wait((2, 0, k), LO)
        t_wait((2, 0, k), HI)
        t_go((2, 0, k), (2, 1, k), pair)

    for k in range(1, NZ):
        t_go((0, 0, 0), (0, 0, k), at(a, zs[k], c))
    spread(0)
    t_wait((0, 0, 1))
    spread(1)
    relay(0)
    t_wait((0, 0, 2))
    spread(2)
    relay(1)
    t_wait((0, 0, 3))
    spread(3)
    relay(2)
    for k in range(2):
        for label in ((0, 1, k), (3, 0, k), (1, 0, k)):
            if label[1]:
                t_wait(label)
            expand(label)
    relay(3)
    relayed(0)
    relayed(1)
    for k in range(2):
        for label in ((3, 1, k), (1, 1, k), (2, 0, k), (0, 1, k + 2), (3, 0, k + 2), (1, 0, k + 2)):
            if label[1]:
                t_wait(label)
            expand(label)
    relayed(2)
    relayed(3)
    for label in ((3, 1, 2), (1, 1, 2), (3, 1, 3), (1, 1, 3), (2, 1, 0), (2, 1, 1), (2, 0, 2), (2, 0, 3), (2, 1, 2), (2, 1, 3)):
        if label[1]:
            t_wait(label)
        expand(label)

    for copy in started + z_copies:
        copy.wait_send()

    norm = jnp.sqrt(jnp.sum(sq[...], keepdims=True))
    scale = 0.25 * (norm + DAMP * norm)
    inverse = 1.0 / scale
    damp = DAMP * norm * inverse
    root0 = lax.rsqrt(jnp.sqrt(scale))

    own_rows = gx[0:XG, 0:W]
    x[0:XG, :] = own_rows.astype(F32)
    xb[0, 0:XG, :] = own_rows
    row_ids = lax.broadcasted_iota(jnp.int32, (XR - XG, W), 0)
    col_ids = lax.broadcasted_iota(jnp.int32, (XR - XG, W), 1)
    unit = ((col_ids == row_ids + OWN * dp) & (row_ids < OWN)).astype(F32)
    x[XG:XR, :] = unit
    xb[0, XG:XR, :] = unit.astype(BF)

    def moment(source, count):
        product = jnp.dot(xb[source, 0:count, :], full[...], preferred_element_type=F32)
        return product * inverse + damp * x[0:count, :]

    def step(source, target, first):
        m = moment(source, XR)
        new_g = 1.25 * x[0:XG, :] - 0.25 * m[0:XG]
        if first:
            new_e = m[XG:XR]
            t_ref[...] = new_g
        else:
            new_e = 1.25 * x[XG:XR, :] - 0.25 * m[XG:XR]
        x[0:XG, :] = new_g
        x[XG:XR, :] = new_e
        xb[target, 0:XG, :] = new_g.astype(BF)
        xb[target, XG:XR, :] = new_e.astype(BF)

    step(0, 1, True)

    def middle(s, carry):
        step((s + 1) % 2, s % 2, False)
        return carry

    lax.fori_loop(0, 4, middle, 0)

    p = 1.25 * t_ref[...] - 0.25 * moment(1, XG)
    t_ref[...] = p
    total = jnp.sum(jnp.sum((p * p).reshape(XG // 8, 8, W), axis=0), keepdims=True) * (root0 * root0)

    def layer_start(n, buffer, peers):
        for k, to in enumerate(peers):
            remote(buffer.at[0], buffer.at[k + 1], r_send.at[n], r_recv.at[n], to).start()

    def layer_wait(n, buffer, count):
        others = buffer.at[pl.ds(1, count)]
        everything = remote(others, others, r_send.at[n], r_recv.at[n], pair)
        everything.wait_recv()
        everything.wait_send()

    red1[0] = jnp.broadcast_to(total, (1, T))
    layer_start(0, red1, [((dp + k) % n_dp, tensor) for k in range(1, n_dp)])
    res_ref[...] = x[XG : XG + OWN, 0:BLK] - unit[0:OWN, 0:BLK]
    layer_wait(0, red1, n_dp - 1)
    red2[0] = jnp.sum(red1[...], axis=0)
    layer_start(1, red2, [(dp, (tensor + k) % n_tensor) for k in range(1, n_tensor)])
    layer_wait(1, red2, n_tensor - 1)
    layer = jnp.sum(red2[...], axis=0)[:, 0:1]
    ratio = math.sqrt(D * FF) / jnp.sqrt(layer + EPSILON) * root0
    upd_ref[...] = (t_ref[0:ROWS, 0:BLK] * ratio).astype(BF)


def body(n_dp, n_tensor, gradient):
    dma = pltpu.SemaphoreType.DMA
    return pl.pallas_call(
        functools.partial(kernel, n_dp, n_tensor),
        out_shape=(
            jax.ShapeDtypeStruct((ROWS, BLK), BF),
            jax.ShapeDtypeStruct((OWN, BLK), F32),
        ),
        in_specs=[pl.BlockSpec(memory_space=pl.ANY)],
        out_specs=(pl.BlockSpec(memory_space=pltpu.VMEM), pl.BlockSpec(memory_space=pltpu.VMEM)),
        scratch_shapes=[
            pltpu.VMEM((ROWS, BLK), BF),
            pltpu.VMEM((KD, EXT * T), BF),
            pltpu.VMEM((8 * KD, (NEED + 1) * T), BF),
            pltpu.VMEM((3, T, HALF * T), F32),
            pltpu.VMEM((12, T, T), BF),
            pltpu.VMEM((NZ - 1, CH, T, T), BF),
            pltpu.VMEM((96, T, T), BF),
            pltpu.VMEM((W, W), BF),
            pltpu.VMEM((XR, W), F32),
            pltpu.VMEM((2, XR, W), BF),
            pltpu.VMEM((XG, W), F32),
            pltpu.VMEM((8, T), F32),
            pltpu.VMEM((n_dp, 1, T), F32),
            pltpu.VMEM((n_tensor, 1, T), F32),
            dma,
            dma((13,)),
            dma((13,)),
            dma((NZ - 1,)),
            dma((NZ - 1,)),
            dma((64,)),
            dma((64,)),
            dma((2,)),
            dma((2,)),
        ],
        compiler_params=pltpu.CompilerParams(
            collective_id=0, has_side_effects=True, vmem_limit_bytes=48 * 1024 * 1024
        ),
        cost_estimate=pl.CostEstimate(flops=6_000_000_000, bytes_accessed=1_000_000, transcendentals=0),
    )(gradient)


def solution(mesh):
    return jax.shard_map(
        functools.partial(body, mesh.shape["dp"], mesh.shape["tensor"]),
        mesh=mesh,
        in_specs=(P("dp", "tensor"),),
        out_specs=(P("dp", "tensor"), P("dp", "tensor")),
        check_vma=False,
    )
```

```python
import functools
import math

import jax
import jax.numpy as jnp
from jax import lax
from jax.experimental import pallas as pl
from jax.experimental.pallas import tpu as pltpu
from jax.sharding import PartitionSpec as P

D = 3200
FF = 12800
BLK = 1600
DAMP = 0.002
EPSILON = 1e-06

T = 128
NB = 13
W = NB * T
HALF = 7
NEED = 10
EXT = 20
KD = 112
ROWS = 100
OWN = 50
XG = 104
XR = 160
NY, NZ, NC = 4, 4, 2
CH = 3
BF = jnp.bfloat16
F32 = jnp.float32
MESH = pl.DeviceIdType.MESH


def band_of(q):
    return q // HALF


def kernel(
    n_dp,
    n_tensor,
    g_hbm,
    upd_ref,
    res_ref,
    g_ref,
    gx,
    gall,
    acc,
    part,
    zrecv,
    tri,
    full,
    x,
    xb,
    t_ref,
    sq,
    red1,
    red2,
    in_sem,
    g_send,
    g_recv,
    z_send,
    z_recv,
    t_send,
    t_recv,
    r_send,
    r_recv,
):
    dp = lax.axis_index("dp")
    tensor = lax.axis_index("tensor")
    a, b, c = dp // (NZ * NC), (dp // NC) % NZ, dp % NC

    def at(a_, b_, c_):
        return ((a_ * NZ + b_) * NC + c_, tensor)

    a_up, a_down = (a + 1) % NY, (a + NY - 1) % NY
    up = at(a_up, b, c)
    down = at(a_down, b, c)
    pair = at(a, b, 1 - c)
    zs = (b, b + 1 - 2 * (b % 2), (b + 2) % NZ, NZ - 1 - b)

    barrier = pltpu.get_barrier_semaphore()
    greeted = [up, down, pair] + [at(a, zs[k], c) for k in range(1, NZ)]
    greeted += [(dp, (tensor + k) % n_tensor) for k in range(1, n_tensor)]
    for to in greeted:
        pl.semaphore_signal(barrier, inc=1, device_id=to, device_id_type=MESH)

    load = pltpu.make_async_copy(g_hbm, g_ref, in_sem)
    load.start()

    def lanes(first, count):
        return pl.ds(pl.multiple_of(first * T, T), count * T)

    def rows(ra, rc):
        return pl.ds((2 * ra + rc) * KD, KD)

    tail = slice(ROWS - ROWS % 16, KD)
    gx[tail, :] = jnp.zeros((KD - tail.start, EXT * T), BF)
    gx[:, BLK - BLK % T : W] = jnp.zeros((KD, T), BF)
    gall[:, NEED * T :] = jnp.zeros((8 * KD, T), BF)
    sq[...] = jnp.zeros_like(sq)
    load.wait()
    gx[0:ROWS, 0:BLK] = g_ref[...]
    gx[0:ROWS, W:] = g_ref[:, 0 : EXT * T - W]

    first_band = [band_of(24 * v) for v in (a, a_up, a_down)]
    gall[0:KD, 0 : NEED * T] = gx[:, lanes(first_band[0], NEED)]
    d_up = (first_band[1] + NB - first_band[0]) % NB
    d_down = (first_band[0] + NB - first_band[2]) % NB

    pl.semaphore_wait(barrier, len(greeted))

    def remote(src, dst, send, recv, to):
        return pltpu.make_async_remote_copy(
            src_ref=src, dst_ref=dst, send_sem=send, recv_sem=recv, device_id=to, device_id_type=MESH
        )

    started = []

    labels = [
        (3, 0, 3, 6),
        (1, 0, 1, 6),
        (3, 0, 0, 3),
        (3, 0, 9, 1),
        (1, 0, 0, 1),
        (1, 0, 7, 3),
        (2, 0, 0, 5),
        (2, 0, 5, 5),
        (0, 1, 0, NEED),
        (3, 1, 0, NEED),
        (1, 1, 0, NEED),
        (2, 1, 0, 5),
        (2, 1, 5, 5),
    ]

    def g_copy(n, src, to):
        ra, rc, first, count = labels[n]
        dst = gall.at[rows(ra, rc), pl.ds(first * T, count * T)]
        return remote(dst if src is None else src, dst, g_send.at[n], g_recv.at[n], to)

    def g_go(n, src, to):
        copy = g_copy(n, src, to)
        copy.start()
        started.append(copy)

    def g_own(n, base, to):
        g_go(n, gx.at[:, lanes(base + labels[n][2], labels[n][3])], to)

    def g_held(n, slot, first, to):
        g_go(n, gall.at[rows(*slot), lanes(first, labels[n][3])], to)

    def g_wait(n):
        g_copy(n, None, pair).wait_recv()

    q0 = 24 * a + 12 * c
    row0 = band_of(q0)
    local0 = row0 - first_band[0]

    def accumulate(start, count, first):
        for m in range(3):
            band = local0 + m
            value = lax.dot_general(
                gall[pl.ds(start, count), lanes(band, 1)],
                gall[pl.ds(start, count), lanes(band, HALF)],
                (((0,), (0,)), ((), ())),
                preferred_element_type=F32,
            )
            acc[m] = value if first else acc[m] + value

    g_own(0, first_band[1], up)
    g_own(1, first_band[2], down)
    g_held(8, (0, 0), 0, pair)
    g_own(2, first_band[1], up)
    g_own(4, first_band[2], down)
    g_own(3, first_band[1], up)
    g_own(5, first_band[2], down)
    g_wait(8)
    accumulate(0, 2 * KD, True)
    g_wait(0)
    g_held(6, (3, 0), d_up, up)
    g_wait(1)
    g_held(7, (1, 0), 5 - d_down, down)
    g_wait(2)
    g_wait(3)
    g_held(9, (3, 0), 0, pair)
    g_wait(4)
    g_wait(5)
    g_held(10, (1, 0), 0, pair)
    g_wait(9)
    accumulate(6 * KD, 2 * KD, False)
    g_wait(10)
    accumulate(2 * KD, 2 * KD, False)
    g_wait(6)
    g_held(11, (2, 0), 0, pair)
    g_wait(7)
    g_held(12, (2, 0), 5, pair)
    accumulate(4 * KD, KD, False)
    g_wait(11)
    g_wait(12)
    accumulate(5 * KD, KD, False)

    def held_tile(e):
        q = q0 + e
        return acc[band_of(q) - row0, :, lanes(q % HALF, 1)]

    def place(label, e):
        ra, rc, k = label
        return 24 * ((a + ra) % NY) + 12 * (c if rc == 0 else 1 - c) + CH * zs[k] + e

    def slot(label, e):
        ra, rc, k = label
        return 48 + ra * NZ + k if rc else (ra * NZ + k) * CH + e

    ALL, LO, HI = pl.ds(0, T), pl.ds(0, T // 2), pl.ds(T // 2, T // 2)
    sent = [0]

    def t_go(held, label, e, to, piece=ALL):
        tile = tri.at[place(held, e), piece, :]
        remote(tile, tile, t_send, t_recv.at[slot(label, e)], to).start()
        sent[0] += piece.size

    def t_wait(label, e):
        tiles = tri.at[place(label, e)] if label[1] == 0 else tri.at[pl.ds(place(label, 0), CH)]
        remote(tiles, tiles, t_send, t_recv.at[slot(label, e)], pair).wait_recv()

    def expand(label):
        first = place(label, 0)

        def tile(e, carry):
            q = first + e

            @pl.when(q < NB * HALF)
            def _():
                i = band_of(q)
                j = (i + q % HALF) % NB
                value = tri[q]
                wide = value.astype(F32)
                weight = jnp.where(q % HALF == 0, 1.0, 2.0)
                sq[...] += weight * jnp.sum((wide * wide).reshape(T // 8, 8, T), axis=0)
                full[lanes(j, 1), lanes(i, 1)] = value.T
                full[lanes(i, 1), lanes(j, 1)] = value

            return carry

        lax.fori_loop(0, CH, tile, 0)

    def z_sum(e):
        remote(zrecv.at[e], zrecv.at[e], z_send, z_recv.at[e], pair).wait_recv()
        total = held_tile(CH * b + e)
        for k in range(NZ - 1):
            total = total + zrecv[e, k].astype(F32)
        tri[place((0, 0, 0), e)] = total.astype(BF)
        for k in range(1, NZ):
            t_go((0, 0, 0), (0, 0, k), e, at(a, zs[k], c))
        spread(0, e)

    def spread(k, e):
        t_go((0, 0, k), (3, 0, k), e, up)
        t_go((0, 0, k), (1, 0, k), e, down)
        t_go((0, 0, k), (0, 1, k), e, pair)

    def z_tile(k, e):
        t_wait((0, 0, k), e)
        spread(k, e)

    def relay(k, e):
        t_wait((3, 0, k), e)
        t_go((3, 0, k), (2, 0, k), e, up, LO)
        t_go((3, 0, k), (3, 1, k), e, pair)
        t_wait((1, 0, k), e)
        t_go((1, 0, k), (2, 0, k), e, down, HI)
        t_go((1, 0, k), (1, 1, k), e, pair)

    def relayed(k, e):
        t_wait((2, 0, k), e)
        t_go((2, 0, k), (2, 1, k), e, pair)

    def from_pair(ra, k):
        t_wait((ra, 1, k), 0)
        expand((ra, 1, k))

    for e in range(CH):
        for k in range(1, NZ):
            part[e, k - 1] = held_tile(CH * zs[k] + e).astype(BF)
            remote(
                part.at[e, k - 1], zrecv.at[e, k - 1], z_send, z_recv.at[e], at(a, zs[k], c)
            ).start()
    z_sum(0)
    z_tile(1, 0)
    z_sum(1)
    relay(0, 0)
    z_tile(1, 1)
    z_tile(2, 0)
    z_tile(3, 0)
    z_sum(2)
    relay(1, 0)
    relay(0, 1)
    relayed(0, 0)
    z_tile(2, 1)
    z_tile(3, 1)
    relay(2, 0)
    relay(3, 0)
    relay(1, 1)
    z_tile(1, 2)
    relay(0, 2)
    expand((0, 0, 0))
    expand((0, 0, 1))
    relayed(1, 0)
    relayed(0, 1)
    z_tile(2, 2)
    z_tile(3, 2)
    relay(2, 1)
    relay(3, 1)
    relay(1, 2)
    expand((3, 0, 0))
    expand((1, 0, 0))
    relayed(2, 0)
    relayed(3, 0)
    relayed(1, 1)
    relayed(0, 2)
    relay(2, 2)
    relay(3, 2)
    expand((0, 0, 2))
    expand((0, 0, 3))
    expand((3, 0, 1))
    expand((1, 0, 1))
    expand((2, 0, 0))
    expand((3, 0, 2))
    expand((1, 0, 2))
    expand((3, 0, 3))
    expand((1, 0, 3))
    from_pair(0, 0)
    from_pair(0, 1)
    relayed(2, 1)
    relayed(3, 1)
    relayed(1, 2)
    from_pair(0, 2)
    from_pair(0, 3)
    from_pair(3, 0)
    from_pair(1, 0)
    from_pair(3, 1)
    from_pair(1, 1)
    expand((2, 0, 1))
    relayed(2, 2)
    relayed(3, 2)
    from_pair(2, 0)
    from_pair(2, 1)
    from_pair(3, 2)
    from_pair(1, 2)
    from_pair(3, 3)
    from_pair(1, 3)
    expand((2, 0, 2))
    expand((2, 0, 3))
    from_pair(2, 2)
    from_pair(2, 3)
    assert sent[0] == 93 * T
    remote(tri.at[pl.ds(0, 93)], tri.at[pl.ds(0, 93)], t_send, t_recv.at[0], pair).wait_send()
    remote(zrecv, zrecv, z_send, z_recv.at[0], pair).wait_send()
    for copy in started:
        copy.wait_send()

    norm = jnp.sqrt(jnp.sum(sq[...], keepdims=True))
    scale = 0.25 * (norm + DAMP * norm)
    inverse = 1.0 / scale
    damp = DAMP * norm * inverse
    root0 = lax.rsqrt(jnp.sqrt(scale))

    def moment(rows, xf, source):
        product = jnp.dot(xb[source, rows, :], full[...], preferred_element_type=F32)
        return product * inverse + damp * xf

    def affine(rows, source, target):
        old = x[rows, :]
        new = 1.25 * old - 0.25 * moment(rows, old, source)
        x[rows, :] = new
        xb[target, rows, :] = new.astype(BF)

    def quartic(rows):
        def step(s, carry):
            affine(rows, (s + 1) % 2, s % 2)
            return carry

        lax.fori_loop(0, 4, step, 0)

    G, E = pl.ds(0, XG), pl.ds(XG, XR - XG)
    own_rows = gx[0:XG, 0:W]
    xb[0, G, :] = own_rows
    x[G, :] = own_rows.astype(F32)
    affine(G, 0, 1)
    t_ref[...] = x[G, :]
    quartic(G)
    p = 1.25 * t_ref[...] - 0.25 * moment(G, x[G, :], 1)
    t_ref[...] = p
    total = jnp.sum(jnp.sum((p * p).reshape(XG // 8, 8, W), axis=0), keepdims=True) * (root0 * root0)

    def layer_start(n, buffer, peers):
        for k, to in enumerate(peers):
            remote(buffer.at[0], buffer.at[k + 1], r_send.at[n], r_recv.at[n], to).start()

    def layer_wait(n, buffer, count):
        others = buffer.at[pl.ds(1, count)]
        everything = remote(others, others, r_send.at[n], r_recv.at[n], pair)
        everything.wait_recv()
        everything.wait_send()

    red1[0] = jnp.broadcast_to(total, (1, T))
    layer_start(0, red1, [((dp + k) % n_dp, tensor) for k in range(1, n_dp)])
    row_ids = lax.broadcasted_iota(jnp.int32, (XR - XG, W), 0)
    col_ids = lax.broadcasted_iota(jnp.int32, (XR - XG, W), 1)
    unit = ((col_ids == row_ids + OWN * dp) & (row_ids < OWN)).astype(F32)
    xb[0, E, :] = unit.astype(BF)
    start = moment(E, unit, 0)
    x[E, :] = start
    xb[1, E, :] = start.astype(BF)
    quartic(E)
    res_ref[...] = x[XG : XG + OWN, 0:BLK] - unit[0:OWN, 0:BLK]
    layer_wait(0, red1, n_dp - 1)
    red2[0] = jnp.sum(red1[...], axis=0)
    layer_start(1, red2, [(dp, (tensor + k) % n_tensor) for k in range(1, n_tensor)])
    layer_wait(1, red2, n_tensor - 1)
    layer = jnp.sum(red2[...], axis=0)[:, 0:1]
    ratio = math.sqrt(D * FF) / jnp.sqrt(layer + EPSILON) * root0
    upd_ref[...] = (t_ref[0:ROWS, 0:BLK] * ratio).astype(BF)


def body(n_dp, n_tensor, gradient):
    dma = pltpu.SemaphoreType.DMA
    return pl.pallas_call(
        functools.partial(kernel, n_dp, n_tensor),
        out_shape=(
            jax.ShapeDtypeStruct((ROWS, BLK), BF),
            jax.ShapeDtypeStruct((OWN, BLK), F32),
        ),
        in_specs=[pl.BlockSpec(memory_space=pl.ANY)],
        out_specs=(pl.BlockSpec(memory_space=pltpu.VMEM), pl.BlockSpec(memory_space=pltpu.VMEM)),
        scratch_shapes=[
            pltpu.VMEM((ROWS, BLK), BF),
            pltpu.VMEM((KD, EXT * T), BF),
            pltpu.VMEM((8 * KD, (NEED + 1) * T), BF),
            pltpu.VMEM((3, T, HALF * T), F32),
            pltpu.VMEM((CH, NZ - 1, T, T), BF),
            pltpu.VMEM((CH, NZ - 1, T, T), BF),
            pltpu.VMEM((96, T, T), BF),
            pltpu.VMEM((W, W), BF),
            pltpu.VMEM((XR, W), F32),
            pltpu.VMEM((2, XR, W), BF),
            pltpu.VMEM((XG, W), F32),
            pltpu.VMEM((8, T), F32),
            pltpu.VMEM((n_dp, 1, T), F32),
            pltpu.VMEM((n_tensor, 1, T), F32),
            dma,
            dma((13,)),
            dma((13,)),
            dma,
            dma((CH,)),
            dma,
            dma((64,)),
            dma((2,)),
            dma((2,)),
        ],
        compiler_params=pltpu.CompilerParams(
            collective_id=0, has_side_effects=True, vmem_limit_bytes=48 * 1024 * 1024
        ),
        cost_estimate=pl.CostEstimate(flops=6_000_000_000, bytes_accessed=1_000_000, transcendentals=0),
    )(gradient)


def solution(mesh):
    return jax.shard_map(
        functools.partial(body, mesh.shape["dp"], mesh.shape["tensor"]),
        mesh=mesh,
        in_specs=(P("dp", "tensor"),),
        out_specs=(P("dp", "tensor"), P("dp", "tensor")),
        check_vma=False,
    )
```

```python
import functools
import math

import jax
import jax.numpy as jnp
from jax import lax
from jax.experimental import pallas as pl
from jax.experimental.pallas import tpu as pltpu
from jax.sharding import PartitionSpec as P

D = 3200
FF = 12800
BLK = 1600
DAMP = 0.002
EPSILON = 1e-06

T = 128
NB = 13
W = NB * T
HALF = 7
NEED = 10
EXT = 20
KD = 112
ROWS = 100
OWN = 50
XG = 104
XR = 160
NY, NZ, NC = 4, 4, 2
CH = 3
BF = jnp.bfloat16
F32 = jnp.float32
MESH = pl.DeviceIdType.MESH


def band_of(q):
    return q // HALF


def kernel(
    n_dp,
    n_tensor,
    g_hbm,
    upd_ref,
    res_ref,
    g_ref,
    gx,
    gall,
    acc,
    part,
    zrecv,
    tri,
    full,
    x,
    xb,
    t_ref,
    sq,
    red1,
    red2,
    in_sem,
    g_send,
    g_recv,
    z_send,
    z_recv,
    t_send,
    t_recv,
    r_send,
    r_recv,
):
    dp = lax.axis_index("dp")
    tensor = lax.axis_index("tensor")
    a, b, c = dp // (NZ * NC), (dp // NC) % NZ, dp % NC

    def at(a_, b_, c_):
        return ((a_ * NZ + b_) * NC + c_, tensor)

    a_up, a_down = (a + 1) % NY, (a + NY - 1) % NY
    up = at(a_up, b, c)
    down = at(a_down, b, c)
    pair = at(a, b, 1 - c)
    zs = (b, b + 1 - 2 * (b % 2), (b + 2) % NZ, NZ - 1 - b)

    barrier = pltpu.get_barrier_semaphore()
    greeted = [up, down, pair] + [at(a, zs[k], c) for k in range(1, NZ)]
    greeted += [(dp, (tensor + k) % n_tensor) for k in range(1, n_tensor)]
    for to in greeted:
        pl.semaphore_signal(barrier, inc=1, device_id=to, device_id_type=MESH)

    load = pltpu.make_async_copy(g_hbm, g_ref, in_sem)
    load.start()

    def lanes(first, count):
        return pl.ds(pl.multiple_of(first * T, T), count * T)

    def rows(ra, rc):
        return pl.ds((2 * ra + rc) * KD, KD)

    tail = slice(ROWS - ROWS % 16, KD)
    gx[tail, :] = jnp.zeros((KD - tail.start, EXT * T), BF)
    gx[:, BLK - BLK % T : W] = jnp.zeros((KD, T), BF)
    gall[:, NEED * T :] = jnp.zeros((8 * KD, T), BF)
    sq[...] = jnp.zeros_like(sq)
    load.wait()
    gx[0:ROWS, 0:BLK] = g_ref[...]
    gx[0:ROWS, W:] = g_ref[:, 0 : EXT * T - W]

    first_band = [band_of(24 * v) for v in (a, a_up, a_down)]
    gall[0:KD, 0 : NEED * T] = gx[:, lanes(first_band[0], NEED)]
    d_up = (first_band[1] + NB - first_band[0]) % NB
    d_down = (first_band[0] + NB - first_band[2]) % NB

    pl.semaphore_wait(barrier, len(greeted))

    def remote(src, dst, send, recv, to):
        return pltpu.make_async_remote_copy(
            src_ref=src, dst_ref=dst, send_sem=send, recv_sem=recv, device_id=to, device_id_type=MESH
        )

    started = []

    labels = [
        (3, 0, 3, 6),
        (1, 0, 1, 6),
        (3, 0, 0, 3),
        (3, 0, 9, 1),
        (1, 0, 0, 1),
        (1, 0, 7, 3),
        (2, 0, 0, 5),
        (2, 0, 5, 5),
        (0, 1, 0, NEED),
        (3, 1, 0, NEED),
        (1, 1, 0, NEED),
        (2, 1, 0, 5),
        (2, 1, 5, 5),
    ]

    def g_copy(n, src, to):
        ra, rc, first, count = labels[n]
        dst = gall.at[rows(ra, rc), pl.ds(first * T, count * T)]
        return remote(dst if src is None else src, dst, g_send.at[n], g_recv.at[n], to)

    def g_go(n, src, to):
        copy = g_copy(n, src, to)
        copy.start()
        started.append(copy)

    def g_own(n, base, to):
        g_go(n, gx.at[:, lanes(base + labels[n][2], labels[n][3])], to)

    def g_held(n, slot, first, to):
        g_go(n, gall.at[rows(*slot), lanes(first, labels[n][3])], to)

    def g_wait(n):
        g_copy(n, None, pair).wait_recv()

    q0 = 24 * a + 12 * c
    row0 = band_of(q0)
    local0 = row0 - first_band[0]

    def accumulate(start, count, first):
        for m in range(3):
            band = local0 + m
            value = lax.dot_general(
                gall[pl.ds(start, count), lanes(band, 1)],
                gall[pl.ds(start, count), lanes(band, HALF)],
                (((0,), (0,)), ((), ())),
                preferred_element_type=F32,
            )
            acc[m] = value if first else acc[m] + value

    g_own(0, first_band[1], up)
    g_own(1, first_band[2], down)
    g_held(8, (0, 0), 0, pair)
    g_own(2, first_band[1], up)
    g_own(4, first_band[2], down)
    g_own(3, first_band[1], up)
    g_own(5, first_band[2], down)
    g_wait(8)
    accumulate(0, 2 * KD, True)
    g_wait(0)
    g_held(6, (3, 0), d_up, up)
    g_wait(1)
    g_held(7, (1, 0), 5 - d_down, down)
    g_wait(2)
    g_wait(3)
    g_held(9, (3, 0), 0, pair)
    g_wait(4)
    g_wait(5)
    g_held(10, (1, 0), 0, pair)
    g_wait(9)
    accumulate(6 * KD, 2 * KD, False)
    g_wait(10)
    accumulate(2 * KD, 2 * KD, False)
    g_wait(6)
    g_held(11, (2, 0), 0, pair)
    g_wait(7)
    g_held(12, (2, 0), 5, pair)
    accumulate(4 * KD, KD, False)
    g_wait(11)
    g_wait(12)
    accumulate(5 * KD, KD, False)

    def held_tile(e):
        q = q0 + e
        return acc[band_of(q) - row0, :, lanes(q % HALF, 1)]

    def place(label, e):
        ra, rc, k = label
        return 24 * ((a + ra) % NY) + 12 * (c if rc == 0 else 1 - c) + CH * zs[k] + e

    def slot(label, e):
        ra, rc, k = label
        return 48 + ra * NZ + k if rc else (ra * NZ + k) * CH + e

    ALL, LO, HI = pl.ds(0, T), pl.ds(0, T // 2), pl.ds(T // 2, T // 2)
    sent = [0]

    def t_go(held, label, e, to, piece=ALL):
        tile = tri.at[place(held, e), piece, :]
        remote(tile, tile, t_send, t_recv.at[slot(label, e)], to).start()
        sent[0] += piece.size

    def t_wait(label, e):
        tiles = tri.at[place(label, e)] if label[1] == 0 else tri.at[pl.ds(place(label, 0), CH)]
        remote(tiles, tiles, t_send, t_recv.at[slot(label, e)], pair).wait_recv()

    def expand(label):
        first = place(label, 0)

        def tile(e, carry):
            q = first + e

            @pl.when(q < NB * HALF)
            def _():
                i = band_of(q)
                j = (i + q % HALF) % NB
                value = tri[q]
                wide = value.astype(F32)
                weight = jnp.where(q % HALF == 0, 1.0, 2.0)
                sq[...] += weight * jnp.sum((wide * wide).reshape(T // 8, 8, T), axis=0)
                full[lanes(j, 1), lanes(i, 1)] = value.T
                full[lanes(i, 1), lanes(j, 1)] = value

            return carry

        lax.fori_loop(0, CH, tile, 0)

    def z_sum(e):
        remote(zrecv.at[e], zrecv.at[e], z_send, z_recv.at[e], pair).wait_recv()
        total = held_tile(CH * b + e)
        for k in range(NZ - 1):
            total = total + zrecv[e, k].astype(F32)
        tri[place((0, 0, 0), e)] = total.astype(BF)
        for k in range(1, NZ):
            t_go((0, 0, 0), (0, 0, k), e, at(a, zs[k], c))
        spread(0, e)

    def spread(k, e):
        t_go((0, 0, k), (3, 0, k), e, up)
        t_go((0, 0, k), (1, 0, k), e, down)
        t_go((0, 0, k), (0, 1, k), e, pair)

    def z_tile(k, e):
        t_wait((0, 0, k), e)
        spread(k, e)

    def last(k, e):
        return e == 2

    def relay(k, e):
        t_wait((3, 0, k), e)
        t_go((3, 0, k), (2, 0, k), e, up, LO)
        if last(k, e):
            t_go((3, 0, k), (2, 1, k), e, at(a_up, b, 1 - c), LO)
        t_go((3, 0, k), (3, 1, k), e, pair)
        t_wait((1, 0, k), e)
        t_go((1, 0, k), (2, 0, k), e, down, HI)
        if last(k, e):
            t_go((1, 0, k), (2, 1, k), e, at(a_down, b, 1 - c), HI)
        t_go((1, 0, k), (1, 1, k), e, pair)

    def relayed(k, e):
        t_wait((2, 0, k), e)
        if not last(k, e):
            t_go((2, 0, k), (2, 1, k), e, pair)

    def from_pair(ra, k):
        t_wait((ra, 1, k), 0)
        expand((ra, 1, k))

    for e in range(CH):
        for k in range(1, NZ):
            part[e, k - 1] = held_tile(CH * zs[k] + e).astype(BF)
            remote(
                part.at[e, k - 1], zrecv.at[e, k - 1], z_send, z_recv.at[e], at(a, zs[k], c)
            ).start()
    z_sum(0)
    z_tile(1, 0)
    z_sum(1)
    relay(0, 0)
    z_tile(1, 1)
    z_tile(2, 0)
    z_tile(3, 0)
    z_sum(2)
    relay(1, 0)
    relay(0, 1)
    relayed(0, 0)
    z_tile(2, 1)
    z_tile(3, 1)
    relay(2, 0)
    relay(3, 0)
    relay(1, 1)
    z_tile(1, 2)
    relay(0, 2)
    expand((0, 0, 0))
    expand((0, 0, 1))
    relayed(1, 0)
    relayed(0, 1)
    z_tile(2, 2)
    z_tile(3, 2)
    relay(2, 1)
    relay(3, 1)
    relay(1, 2)
    expand((3, 0, 0))
    expand((1, 0, 0))
    relayed(2, 0)
    relayed(3, 0)
    relayed(1, 1)
    relayed(0, 2)
    relay(2, 2)
    relay(3, 2)
    expand((0, 0, 2))
    expand((0, 0, 3))
    expand((3, 0, 1))
    expand((1, 0, 1))
    expand((2, 0, 0))
    expand((3, 0, 2))
    expand((1, 0, 2))
    expand((3, 0, 3))
    expand((1, 0, 3))
    from_pair(0, 0)
    from_pair(0, 1)
    relayed(2, 1)
    relayed(3, 1)
    relayed(1, 2)
    from_pair(0, 2)
    from_pair(0, 3)
    from_pair(3, 0)
    from_pair(1, 0)
    from_pair(3, 1)
    from_pair(1, 1)
    expand((2, 0, 1))
    relayed(2, 2)
    relayed(3, 2)
    from_pair(2, 0)
    from_pair(2, 1)
    from_pair(3, 2)
    from_pair(1, 2)
    from_pair(3, 3)
    from_pair(1, 3)
    expand((2, 0, 2))
    expand((2, 0, 3))
    from_pair(2, 2)
    from_pair(2, 3)
    assert sent[0] == 93 * T
    remote(tri.at[pl.ds(0, 93)], tri.at[pl.ds(0, 93)], t_send, t_recv.at[0], pair).wait_send()
    remote(zrecv, zrecv, z_send, z_recv.at[0], pair).wait_send()
    for copy in started:
        copy.wait_send()

    norm = jnp.sqrt(jnp.sum(sq[...], keepdims=True))
    scale = 0.25 * (norm + DAMP * norm)
    inverse = 1.0 / scale
    damp = DAMP * norm * inverse
    root0 = lax.rsqrt(jnp.sqrt(scale))

    def moment(rows, xf, source):
        product = jnp.dot(xb[source, rows, :], full[...], preferred_element_type=F32)
        return product * inverse + damp * xf

    def affine(rows, source, target):
        old = x[rows, :]
        new = 1.25 * old - 0.25 * moment(rows, old, source)
        x[rows, :] = new
        xb[target, rows, :] = new.astype(BF)

    def affines(rows, count):
        def step(s, carry):
            affine(rows, (s + 1) % 2, s % 2)
            return carry

        lax.fori_loop(0, count, step, 0)

    G, E = pl.ds(0, XG), pl.ds(XG, XR - XG)
    own_rows = gx[0:XG, 0:W]
    xb[0, G, :] = own_rows
    x[G, :] = own_rows.astype(F32)
    affine(G, 0, 1)
    t_ref[...] = x[G, :]
    affines(G, 4)
    p = 1.25 * t_ref[...] - 0.25 * moment(G, x[G, :], 1)
    t_ref[...] = p
    total = jnp.sum(jnp.sum((p * p).reshape(XG // 8, 8, W), axis=0), keepdims=True) * (root0 * root0)

    def layer_start(n, buffer, peers):
        for k, to in enumerate(peers):
            remote(buffer.at[0], buffer.at[k + 1], r_send.at[n], r_recv.at[n], to).start()

    def layer_wait(n, buffer, count):
        others = buffer.at[pl.ds(1, count)]
        everything = remote(others, others, r_send.at[n], r_recv.at[n], pair)
        everything.wait_recv()
        everything.wait_send()

    red1[0] = jnp.broadcast_to(total, (1, T))
    layer_start(0, red1, [((dp + k) % n_dp, tensor) for k in range(1, n_dp)])
    row_ids = lax.broadcasted_iota(jnp.int32, (XR - XG, W), 0)
    col_ids = lax.broadcasted_iota(jnp.int32, (XR - XG, W), 1)
    unit = ((col_ids == row_ids + OWN * dp) & (row_ids < OWN)).astype(F32)
    xb[0, E, :] = unit.astype(BF)
    start = moment(E, unit, 0)
    x[E, :] = start
    xb[1, E, :] = start.astype(BF)
    affines(E, 2)
    layer_wait(0, red1, n_dp - 1)
    red2[0] = jnp.sum(red1[...], axis=0)
    layer_start(1, red2, [(dp, (tensor + k) % n_tensor) for k in range(1, n_tensor)])
    affines(E, 2)
    row_ids = lax.broadcasted_iota(jnp.int32, (OWN, BLK), 0)
    col_ids = lax.broadcasted_iota(jnp.int32, (OWN, BLK), 1)
    res_ref[...] = x[XG : XG + OWN, 0:BLK] - (col_ids == row_ids + OWN * dp).astype(F32)
    layer_wait(1, red2, n_tensor - 1)
    layer = jnp.sum(red2[...], axis=0)[:, 0:1]
    ratio = math.sqrt(D * FF) / jnp.sqrt(layer + EPSILON) * root0
    upd_ref[...] = (t_ref[0:ROWS, 0:BLK] * ratio).astype(BF)


def body(n_dp, n_tensor, gradient):
    dma = pltpu.SemaphoreType.DMA
    return pl.pallas_call(
        functools.partial(kernel, n_dp, n_tensor),
        out_shape=(
            jax.ShapeDtypeStruct((ROWS, BLK), BF),
            jax.ShapeDtypeStruct((OWN, BLK), F32),
        ),
        in_specs=[pl.BlockSpec(memory_space=pl.ANY)],
        out_specs=(pl.BlockSpec(memory_space=pltpu.VMEM), pl.BlockSpec(memory_space=pltpu.VMEM)),
        scratch_shapes=[
            pltpu.VMEM((ROWS, BLK), BF),
            pltpu.VMEM((KD, EXT * T), BF),
            pltpu.VMEM((8 * KD, (NEED + 1) * T), BF),
            pltpu.VMEM((3, T, HALF * T), F32),
            pltpu.VMEM((CH, NZ - 1, T, T), BF),
            pltpu.VMEM((CH, NZ - 1, T, T), BF),
            pltpu.VMEM((96, T, T), BF),
            pltpu.VMEM((W, W), BF),
            pltpu.VMEM((XR, W), F32),
            pltpu.VMEM((2, XR, W), BF),
            pltpu.VMEM((XG, W), F32),
            pltpu.VMEM((8, T), F32),
            pltpu.VMEM((n_dp, 1, T), F32),
            pltpu.VMEM((n_tensor, 1, T), F32),
            dma,
            dma((13,)),
            dma((13,)),
            dma,
            dma((CH,)),
            dma,
            dma((64,)),
            dma((2,)),
            dma((2,)),
        ],
        compiler_params=pltpu.CompilerParams(
            collective_id=0, has_side_effects=True, vmem_limit_bytes=48 * 1024 * 1024
        ),
        cost_estimate=pl.CostEstimate(flops=6_000_000_000, bytes_accessed=1_000_000, transcendentals=0),
    )(gradient)


def solution(mesh):
    return jax.shard_map(
        functools.partial(body, mesh.shape["dp"], mesh.shape["tensor"]),
        mesh=mesh,
        in_specs=(P("dp", "tensor"),),
        out_specs=(P("dp", "tensor"), P("dp", "tensor")),
        check_vma=False,
    )
```

```python
import functools
import math

import jax
import jax.numpy as jnp
from jax import lax
from jax.experimental import pallas as pl
from jax.experimental.pallas import tpu as pltpu
from jax.sharding import PartitionSpec as P

D = 3200
FF = 12800
BLK = 1600
DAMP = 0.002
EPSILON = 1e-06

T = 128
NB = 13
W = NB * T
HALF = 7
NEED = 10
EXT = 20
KD = 112
ROWS = 100
OWN = 50
XG = 104
XR = 160
NY, NZ, NC = 4, 4, 2
CH = 3
BF = jnp.bfloat16
F32 = jnp.float32
MESH = pl.DeviceIdType.MESH


def band_of(q):
    return q // HALF


def kernel(
    n_dp,
    n_tensor,
    g_ref,
    upd_ref,
    res_ref,
    gx,
    gall,
    acc,
    part,
    zrecv,
    tri,
    full,
    x,
    xb,
    t_ref,
    sq,
    red1,
    red2,
    g_send,
    g_recv,
    z_send,
    z_recv,
    t_send,
    t_recv,
    r_send,
    r_recv,
):
    dp = lax.axis_index("dp")
    tensor = lax.axis_index("tensor")
    a, b, c = dp // (NZ * NC), (dp // NC) % NZ, dp % NC

    def at(a_, b_, c_):
        return ((a_ * NZ + b_) * NC + c_, tensor)

    a_up, a_down = (a + 1) % NY, (a + NY - 1) % NY
    up = at(a_up, b, c)
    down = at(a_down, b, c)
    pair = at(a, b, 1 - c)
    zs = (b, b + 1 - 2 * (b % 2), (b + 2) % NZ, NZ - 1 - b)

    barrier = pltpu.get_barrier_semaphore()
    greeted = [up, down, pair] + [at(a, zs[k], c) for k in range(1, NZ)]
    greeted += [(dp, (tensor + k) % n_tensor) for k in range(1, n_tensor)]
    for to in greeted:
        pl.semaphore_signal(barrier, inc=1, device_id=to, device_id_type=MESH)

    def lanes(first, count):
        return pl.ds(pl.multiple_of(first * T, T), count * T)

    def rows(ra, rc):
        return pl.ds((2 * ra + rc) * KD, KD)

    tail = slice(ROWS - ROWS % 16, KD)
    gx[tail, :] = jnp.zeros((KD - tail.start, EXT * T), BF)
    gx[:, BLK - BLK % T : W] = jnp.zeros((KD, T), BF)
    gx[0:ROWS, 0:BLK] = g_ref[...]
    gx[0:ROWS, W:] = g_ref[:, 0 : EXT * T - W]

    first_band = [band_of(24 * v) for v in (a, a_up, a_down)]
    d_up = (first_band[1] + NB - first_band[0]) % NB
    d_down = (first_band[0] + NB - first_band[2]) % NB

    pl.semaphore_wait(barrier, len(greeted))

    def remote(src, dst, send, recv, to):
        return pltpu.make_async_remote_copy(
            src_ref=src, dst_ref=dst, send_sem=send, recv_sem=recv, device_id=to, device_id_type=MESH
        )

    started = []

    labels = [
        (3, 0, 3, 6),
        (1, 0, 1, 6),
        (3, 0, 0, 3),
        (3, 0, 9, 1),
        (1, 0, 0, 1),
        (1, 0, 7, 3),
        (2, 0, 0, 5),
        (2, 0, 5, 5),
        (0, 1, 0, NEED),
        (3, 1, 0, NEED),
        (1, 1, 0, NEED),
        (2, 1, 0, 5),
        (2, 1, 5, 5),
    ]

    def g_copy(n, src, to):
        ra, rc, first, count = labels[n]
        dst = gall.at[rows(ra, rc), pl.ds(first * T, count * T)]
        return remote(dst if src is None else src, dst, g_send.at[n], g_recv.at[n], to)

    def g_go(n, src, to):
        copy = g_copy(n, src, to)
        copy.start()
        started.append(copy)

    def g_own(n, base, to):
        g_go(n, gx.at[:, lanes(base + labels[n][2], labels[n][3])], to)

    def g_held(n, slot, first, to):
        g_go(n, gall.at[rows(*slot), lanes(first, labels[n][3])], to)

    def g_wait(n):
        g_copy(n, None, pair).wait_recv()

    q0 = 24 * a + 12 * c
    row0 = band_of(q0)
    local0 = row0 - first_band[0]

    def accumulate(start, count, first):
        for m in range(3):
            band = local0 + m
            value = lax.dot_general(
                gall[pl.ds(start, count), lanes(band, 1)],
                gall[pl.ds(start, count), lanes(band, HALF)],
                (((0,), (0,)), ((), ())),
                preferred_element_type=F32,
            )
            acc[m] = value if first else acc[m] + value

    g_own(0, first_band[1], up)
    g_own(1, first_band[2], down)
    g_own(8, first_band[0], pair)
    g_own(2, first_band[1], up)
    g_own(4, first_band[2], down)
    g_own(3, first_band[1], up)
    g_own(5, first_band[2], down)
    gall[0:KD, 0 : NEED * T] = gx[:, lanes(first_band[0], NEED)]
    gall[:, NEED * T :] = jnp.zeros((8 * KD, T), BF)
    sq[...] = jnp.zeros_like(sq)
    G, E = pl.ds(0, XG), pl.ds(XG, XR - XG)
    xb[0, G, :] = gx[0:XG, 0:W]
    x[G, :] = gx[0:XG, 0:W].astype(F32)
    g_wait(8)
    accumulate(0, 2 * KD, True)
    g_wait(0)
    g_held(6, (3, 0), d_up, up)
    g_wait(1)
    g_held(7, (1, 0), 5 - d_down, down)
    g_wait(2)
    g_wait(3)
    g_held(9, (3, 0), 0, pair)
    g_wait(4)
    g_wait(5)
    g_held(10, (1, 0), 0, pair)
    g_wait(9)
    accumulate(6 * KD, 2 * KD, False)
    g_wait(10)
    accumulate(2 * KD, 2 * KD, False)
    g_wait(6)
    g_held(11, (2, 0), 0, pair)
    g_wait(7)
    g_held(12, (2, 0), 5, pair)
    accumulate(4 * KD, KD, False)
    g_wait(11)
    g_wait(12)
    accumulate(5 * KD, KD, False)

    def held_tile(e):
        q = q0 + e
        return acc[band_of(q) - row0, :, lanes(q % HALF, 1)]

    def place(label, e):
        ra, rc, k = label
        return 24 * ((a + ra) % NY) + 12 * (c if rc == 0 else 1 - c) + CH * zs[k] + e

    def slot(label, e):
        ra, rc, k = label
        return 48 + ra * NZ + k if rc else (ra * NZ + k) * CH + e

    ALL, LO, HI = pl.ds(0, T), pl.ds(0, T // 2), pl.ds(T // 2, T // 2)
    sent = [0]

    def t_go(held, label, e, to, piece=ALL):
        tile = tri.at[place(held, e), piece, :]
        remote(tile, tile, t_send, t_recv.at[slot(label, e)], to).start()
        sent[0] += piece.size

    def t_wait(label, e):
        tiles = tri.at[place(label, e)] if label[1] == 0 else tri.at[pl.ds(place(label, 0), CH)]
        remote(tiles, tiles, t_send, t_recv.at[slot(label, e)], pair).wait_recv()

    def expand(label):
        first = place(label, 0)

        def tile(e, carry):
            q = first + e

            @pl.when(q < NB * HALF)
            def _():
                i = band_of(q)
                j = (i + q % HALF) % NB
                value = tri[q]
                wide = value.astype(F32)
                weight = jnp.where(q % HALF == 0, 1.0, 2.0)
                sq[...] += weight * jnp.sum((wide * wide).reshape(T // 8, 8, T), axis=0)
                full[lanes(j, 1), lanes(i, 1)] = value.T
                full[lanes(i, 1), lanes(j, 1)] = value

            return carry

        lax.fori_loop(0, CH, tile, 0)

    def z_sum(e):
        remote(zrecv.at[e], zrecv.at[e], z_send, z_recv.at[e], pair).wait_recv()
        total = held_tile(CH * b + e)
        for k in range(NZ - 1):
            total = total + zrecv[e, k].astype(F32)
        tri[place((0, 0, 0), e)] = total.astype(BF)
        for k in range(1, NZ):
            t_go((0, 0, 0), (0, 0, k), e, at(a, zs[k], c))
        spread(0, e)

    def spread(k, e):
        t_go((0, 0, k), (3, 0, k), e, up)
        t_go((0, 0, k), (1, 0, k), e, down)
        t_go((0, 0, k), (0, 1, k), e, pair)

    def z_tile(k, e):
        t_wait((0, 0, k), e)
        spread(k, e)

    def relay(k, e):
        t_wait((3, 0, k), e)
        t_go((3, 0, k), (2, 0, k), e, up, LO)
        t_go((3, 0, k), (3, 1, k), e, pair)
        t_wait((1, 0, k), e)
        t_go((1, 0, k), (2, 0, k), e, down, HI)
        t_go((1, 0, k), (1, 1, k), e, pair)

    def relayed(k, e):
        t_wait((2, 0, k), e)
        t_go((2, 0, k), (2, 1, k), e, pair)

    def from_pair(ra, k):
        t_wait((ra, 1, k), 0)
        expand((ra, 1, k))

    for e in range(CH):
        for k in range(1, NZ):
            part[e, k - 1] = held_tile(CH * zs[k] + e).astype(BF)
            remote(
                part.at[e, k - 1], zrecv.at[e, k - 1], z_send, z_recv.at[e], at(a, zs[k], c)
            ).start()
    z_sum(0)
    z_tile(1, 0)
    z_sum(1)
    relay(0, 0)
    z_tile(1, 1)
    z_tile(2, 0)
    z_tile(3, 0)
    z_sum(2)
    relay(1, 0)
    relay(0, 1)
    relayed(0, 0)
    z_tile(2, 1)
    z_tile(3, 1)
    relay(2, 0)
    relay(3, 0)
    relay(1, 1)
    z_tile(1, 2)
    relay(0, 2)
    expand((0, 0, 0))
    expand((0, 0, 1))
    relayed(1, 0)
    relayed(0, 1)
    z_tile(2, 2)
    z_tile(3, 2)
    relay(2, 1)
    relay(3, 1)
    relay(1, 2)
    expand((3, 0, 0))
    expand((1, 0, 0))
    relayed(2, 0)
    relayed(3, 0)
    relayed(1, 1)
    relayed(0, 2)
    relay(2, 2)
    relay(3, 2)
    expand((0, 0, 2))
    expand((0, 0, 3))
    expand((3, 0, 1))
    expand((1, 0, 1))
    expand((2, 0, 0))
    expand((3, 0, 2))
    expand((1, 0, 2))
    expand((3, 0, 3))
    expand((1, 0, 3))
    from_pair(0, 0)
    from_pair(0, 1)
    relayed(2, 1)
    relayed(3, 1)
    relayed(1, 2)
    from_pair(0, 2)
    from_pair(0, 3)
    from_pair(3, 0)
    from_pair(1, 0)
    from_pair(3, 1)
    from_pair(1, 1)
    expand((2, 0, 1))
    relayed(2, 2)
    relayed(3, 2)
    from_pair(2, 0)
    from_pair(2, 1)
    from_pair(3, 2)
    from_pair(1, 2)
    from_pair(3, 3)
    from_pair(1, 3)
    expand((2, 0, 2))
    expand((2, 0, 3))
    from_pair(2, 2)
    from_pair(2, 3)
    assert sent[0] == 93 * T
    remote(tri.at[pl.ds(0, 93)], tri.at[pl.ds(0, 93)], t_send, t_recv.at[0], pair).wait_send()
    remote(zrecv, zrecv, z_send, z_recv.at[0], pair).wait_send()
    for copy in started:
        copy.wait_send()

    norm = jnp.sqrt(jnp.sum(sq[...], keepdims=True))
    scale = 0.25 * (norm + DAMP * norm)
    inverse = 1.0 / scale
    damp = DAMP * norm * inverse
    root0 = lax.rsqrt(jnp.sqrt(scale))

    def moment(rows, xf, source):
        product = jnp.dot(xb[source, rows, :], full[...], preferred_element_type=F32)
        return product * inverse + damp * xf

    def affine(rows, source, target):
        old = x[rows, :]
        new = 1.25 * old - 0.25 * moment(rows, old, source)
        x[rows, :] = new
        xb[target, rows, :] = new.astype(BF)

    def affines(rows, count):
        def step(s, carry):
            affine(rows, (s + 1) % 2, s % 2)
            return carry

        lax.fori_loop(0, count, step, 0)

    affine(G, 0, 1)
    t_ref[...] = x[G, :]
    affines(G, 4)
    p = 1.25 * t_ref[...] - 0.25 * moment(G, x[G, :], 1)
    t_ref[...] = p
    total = jnp.sum(jnp.sum((p * p).reshape(XG // 8, 8, W), axis=0), keepdims=True) * (root0 * root0)

    def layer_start(n, buffer, peers):
        for k, to in enumerate(peers):
            remote(buffer.at[0], buffer.at[k + 1], r_send.at[n], r_recv.at[n], to).start()

    def layer_wait(n, buffer, count):
        others = buffer.at[pl.ds(1, count)]
        everything = remote(others, others, r_send.at[n], r_recv.at[n], pair)
        everything.wait_recv()
        everything.wait_send()

    red1[0] = jnp.broadcast_to(total, (1, T))
    layer_start(0, red1, [((dp + k) % n_dp, tensor) for k in range(1, n_dp)])
    row_ids = lax.broadcasted_iota(jnp.int32, (XR - XG, W), 0)
    col_ids = lax.broadcasted_iota(jnp.int32, (XR - XG, W), 1)
    unit = ((col_ids == row_ids + OWN * dp) & (row_ids < OWN)).astype(F32)
    xb[0, E, :] = unit.astype(BF)
    start = moment(E, unit, 0)
    x[E, :] = start
    xb[1, E, :] = start.astype(BF)
    affines(E, 2)
    layer_wait(0, red1, n_dp - 1)
    red2[0] = jnp.sum(red1[...], axis=0)
    layer_start(1, red2, [(dp, (tensor + k) % n_tensor) for k in range(1, n_tensor)])
    affines(E, 2)
    row_ids = lax.broadcasted_iota(jnp.int32, (OWN, BLK), 0)
    col_ids = lax.broadcasted_iota(jnp.int32, (OWN, BLK), 1)
    res_ref[...] = x[XG : XG + OWN, 0:BLK] - (col_ids == row_ids + OWN * dp).astype(F32)
    layer_wait(1, red2, n_tensor - 1)
    layer = jnp.sum(red2[...], axis=0)[:, 0:1]
    ratio = math.sqrt(D * FF) / jnp.sqrt(layer + EPSILON) * root0
    upd_ref[...] = (t_ref[0:ROWS, 0:BLK] * ratio).astype(BF)


def body(n_dp, n_tensor, gradient):
    dma = pltpu.SemaphoreType.DMA
    return pl.pallas_call(
        functools.partial(kernel, n_dp, n_tensor),
        out_shape=(
            jax.ShapeDtypeStruct((ROWS, BLK), BF),
            jax.ShapeDtypeStruct((OWN, BLK), F32),
        ),
        in_specs=[pl.BlockSpec(memory_space=pltpu.VMEM)],
        out_specs=(pl.BlockSpec(memory_space=pltpu.VMEM), pl.BlockSpec(memory_space=pltpu.VMEM)),
        scratch_shapes=[
            pltpu.VMEM((KD, EXT * T), BF),
            pltpu.VMEM((8 * KD, (NEED + 1) * T), BF),
            pltpu.VMEM((3, T, HALF * T), F32),
            pltpu.VMEM((CH, NZ - 1, T, T), BF),
            pltpu.VMEM((CH, NZ - 1, T, T), BF),
            pltpu.VMEM((96, T, T), BF),
            pltpu.VMEM((W, W), BF),
            pltpu.VMEM((XR, W), F32),
            pltpu.VMEM((2, XR, W), BF),
            pltpu.VMEM((XG, W), F32),
            pltpu.VMEM((8, T), F32),
            pltpu.VMEM((n_dp, 1, T), F32),
            pltpu.VMEM((n_tensor, 1, T), F32),
            dma((13,)),
            dma((13,)),
            dma,
            dma((CH,)),
            dma,
            dma((64,)),
            dma((2,)),
            dma((2,)),
        ],
        compiler_params=pltpu.CompilerParams(
            collective_id=0, has_side_effects=True, vmem_limit_bytes=48 * 1024 * 1024
        ),
        cost_estimate=pl.CostEstimate(flops=6_000_000_000, bytes_accessed=1_000_000, transcendentals=0),
    )(gradient)


def solution(mesh):
    return jax.shard_map(
        functools.partial(body, mesh.shape["dp"], mesh.shape["tensor"]),
        mesh=mesh,
        in_specs=(P("dp", "tensor"),),
        out_specs=(P("dp", "tensor"), P("dp", "tensor")),
        check_vma=False,
    )
```

```python
import functools
import math

import jax
import jax.numpy as jnp
from jax import lax
from jax.experimental import pallas as pl
from jax.experimental.pallas import tpu as pltpu
from jax.sharding import PartitionSpec as P

D = 3200
FF = 12800
BLK = 1600
DAMP = 0.002
EPSILON = 1e-06

T = 128
NB = 13
W = NB * T
HALF = 7
NEED = 10
EXT = 20
KD = 112
ROWS = 100
OWN = 50
XG = 104
XR = 160
NY, NZ, NC = 4, 4, 2
CH = 3
BF = jnp.bfloat16
F32 = jnp.float32
MESH = pl.DeviceIdType.MESH


def band_of(q):
    return q // HALF


def kernel(
    n_dp,
    n_tensor,
    g_ref,
    upd_ref,
    res_ref,
    gx,
    gall,
    acc,
    part,
    zrecv,
    tri,
    full,
    x,
    xb,
    t_ref,
    sq,
    red1,
    red2,
    g_send,
    g_recv,
    z_send,
    z_recv,
    t_send,
    t_recv,
    r_send,
    r_recv,
):
    dp = lax.axis_index("dp")
    tensor = lax.axis_index("tensor")
    a, b, c = dp // (NZ * NC), (dp // NC) % NZ, dp % NC

    def at(a_, b_, c_):
        return ((a_ * NZ + b_) * NC + c_, tensor)

    a_up, a_down = (a + 1) % NY, (a + NY - 1) % NY
    up = at(a_up, b, c)
    down = at(a_down, b, c)
    pair = at(a, b, 1 - c)
    zs = (b, b + 1 - 2 * (b % 2), (b + 2) % NZ, NZ - 1 - b)

    barrier = pltpu.get_barrier_semaphore()
    greeted = [up, down, pair] + [at(a, zs[k], c) for k in range(1, NZ)]
    greeted += [(dp, (tensor + k) % n_tensor) for k in range(1, n_tensor)]
    for to in greeted:
        pl.semaphore_signal(barrier, inc=1, device_id=to, device_id_type=MESH)

    def lanes(first, count):
        return pl.ds(pl.multiple_of(first * T, T), count * T)

    def rows(ra, rc):
        return pl.ds((2 * ra + rc) * KD, KD)

    tail = slice(ROWS - ROWS % 16, KD)
    gx[tail, :] = jnp.zeros((KD - tail.start, EXT * T), BF)
    gx[:, BLK - BLK % T : W] = jnp.zeros((KD, T), BF)
    gx[0:ROWS, 0:BLK] = g_ref[...]
    gx[0:ROWS, W:] = g_ref[:, 0 : EXT * T - W]

    first_band = [band_of(24 * v) for v in (a, a_up, a_down)]
    d_up = (first_band[1] + NB - first_band[0]) % NB
    d_down = (first_band[0] + NB - first_band[2]) % NB

    pl.semaphore_wait(barrier, len(greeted))

    def remote(src, dst, send, recv, to):
        return pltpu.make_async_remote_copy(
            src_ref=src, dst_ref=dst, send_sem=send, recv_sem=recv, device_id=to, device_id_type=MESH
        )

    started = []

    labels = [
        (3, 0, 3, 6),
        (1, 0, 1, 6),
        (3, 0, 0, 3),
        (3, 0, 9, 1),
        (1, 0, 0, 1),
        (1, 0, 7, 3),
        (2, 0, 0, 5),
        (2, 0, 5, 5),
        (0, 1, 0, NEED),
        (3, 1, 0, NEED),
        (1, 1, 0, NEED),
        (2, 1, 0, 5),
        (2, 1, 5, 5),
    ]

    def g_copy(n, src, to):
        ra, rc, first, count = labels[n]
        dst = gall.at[rows(ra, rc), pl.ds(first * T, count * T)]
        return remote(dst if src is None else src, dst, g_send.at[n], g_recv.at[n], to)

    def g_go(n, src, to):
        copy = g_copy(n, src, to)
        copy.start()
        started.append(copy)

    def g_own(n, base, to):
        g_go(n, gx.at[:, lanes(base + labels[n][2], labels[n][3])], to)

    def g_held(n, slot, first, to):
        g_go(n, gall.at[rows(*slot), lanes(first, labels[n][3])], to)

    def g_wait(n):
        g_copy(n, None, pair).wait_recv()

    q0 = 24 * a + 12 * c
    row0 = band_of(q0)
    local0 = row0 - first_band[0]

    def accumulate(start, count, first):
        for m in range(3):
            band = local0 + m
            value = lax.dot_general(
                gall[pl.ds(start, count), lanes(band, 1)],
                gall[pl.ds(start, count), lanes(band, HALF)],
                (((0,), (0,)), ((), ())),
                preferred_element_type=F32,
            )
            acc[m] = value if first else acc[m] + value

    g_own(0, first_band[1], up)
    g_own(1, first_band[2], down)
    g_own(8, first_band[0], pair)
    g_own(2, first_band[1], up)
    g_own(4, first_band[2], down)
    g_own(3, first_band[1], up)
    g_own(5, first_band[2], down)
    gall[0:KD, 0 : NEED * T] = gx[:, lanes(first_band[0], NEED)]
    gall[:, NEED * T :] = jnp.zeros((8 * KD, T), BF)
    sq[...] = jnp.zeros_like(sq)
    G, E = pl.ds(0, XG), pl.ds(XG, XR - XG)
    xb[0, G, :] = gx[0:XG, 0:W]
    x[G, :] = gx[0:XG, 0:W].astype(F32)
    g_wait(8)
    accumulate(0, 2 * KD, True)
    g_wait(0)
    g_held(6, (3, 0), d_up, up)
    g_wait(1)
    g_held(7, (1, 0), 5 - d_down, down)
    g_wait(2)
    g_wait(3)
    g_held(9, (3, 0), 0, pair)
    g_wait(4)
    g_wait(5)
    g_held(10, (1, 0), 0, pair)
    g_wait(9)
    accumulate(6 * KD, 2 * KD, False)
    g_wait(10)
    accumulate(2 * KD, 2 * KD, False)
    g_wait(6)
    g_held(11, (2, 0), 0, pair)
    g_wait(7)
    g_held(12, (2, 0), 5, pair)
    accumulate(4 * KD, KD, False)
    g_wait(11)
    g_wait(12)
    accumulate(5 * KD, KD, False)

    def held_tile(e):
        q = q0 + e
        return acc[band_of(q) - row0, :, lanes(q % HALF, 1)]

    def place(label, e):
        ra, rc, k = label
        return 24 * ((a + ra) % NY) + 12 * (c if rc == 0 else 1 - c) + CH * zs[k] + e

    def slot(label, e):
        ra, rc, k = label
        return 48 + ra * NZ + k if rc else (ra * NZ + k) * CH + e

    ALL, LO, HI = pl.ds(0, T), pl.ds(0, T // 2), pl.ds(T // 2, T // 2)
    sent = [0]

    def t_go(held, label, e, to, piece=ALL):
        tile = tri.at[place(held, e), piece, :]
        remote(tile, tile, t_send, t_recv.at[slot(label, e)], to).start()
        sent[0] += piece.size

    def t_wait(label, e):
        tiles = tri.at[place(label, e)] if label[1] == 0 else tri.at[pl.ds(place(label, 0), CH)]
        remote(tiles, tiles, t_send, t_recv.at[slot(label, e)], pair).wait_recv()

    def expand(label):
        first = place(label, 0)

        def tile(e, carry):
            q = first + e

            @pl.when(q < NB * HALF)
            def _():
                i = band_of(q)
                j = (i + q % HALF) % NB
                value = tri[q]
                wide = value.astype(F32)
                weight = jnp.where(q % HALF == 0, 1.0, 2.0)
                sq[...] += weight * jnp.sum((wide * wide).reshape(T // 8, 8, T), axis=0)
                full[lanes(j, 1), lanes(i, 1)] = value.T
                full[lanes(i, 1), lanes(j, 1)] = value

            return carry

        lax.fori_loop(0, CH, tile, 0)

    def z_sum(e):
        remote(zrecv.at[e], zrecv.at[e], z_send, z_recv.at[e], pair).wait_recv()
        total = held_tile(CH * b + e)
        for k in range(NZ - 1):
            total = total + zrecv[e, k].astype(F32)
        tri[place((0, 0, 0), e)] = total.astype(BF)
        for k in range(1, NZ):
            t_go((0, 0, 0), (0, 0, k), e, at(a, zs[k], c))
        spread(0, e)

    def spread(k, e):
        t_go((0, 0, k), (3, 0, k), e, up)
        t_go((0, 0, k), (1, 0, k), e, down)
        t_go((0, 0, k), (0, 1, k), e, pair)

    def z_tile(k, e):
        t_wait((0, 0, k), e)
        spread(k, e)

    def relay(k, e):
        t_wait((3, 0, k), e)
        t_go((3, 0, k), (2, 0, k), e, up, LO)
        t_go((3, 0, k), (3, 1, k), e, pair)
        t_wait((1, 0, k), e)
        t_go((1, 0, k), (2, 0, k), e, down, HI)
        t_go((1, 0, k), (1, 1, k), e, pair)

    def relayed(k, e):
        t_wait((2, 0, k), e)
        t_go((2, 0, k), (2, 1, k), e, pair)

    def from_pair(ra, k):
        t_wait((ra, 1, k), 0)
        expand((ra, 1, k))

    for e in range(CH):
        for k in (2, 3, 1):
            part[e, k - 1] = held_tile(CH * zs[k] + e).astype(BF)
            remote(
                part.at[e, k - 1], zrecv.at[e, k - 1], z_send, z_recv.at[e], at(a, zs[k], c)
            ).start()
    z_sum(0)
    z_tile(1, 0)
    z_sum(1)
    relay(0, 0)
    z_tile(1, 1)
    z_tile(2, 0)
    z_tile(3, 0)
    z_sum(2)
    relay(1, 0)
    relay(0, 1)
    relayed(0, 0)
    z_tile(2, 1)
    z_tile(3, 1)
    relay(2, 0)
    relay(3, 0)
    relay(1, 1)
    z_tile(1, 2)
    relay(0, 2)
    expand((0, 0, 0))
    expand((0, 0, 1))
    relayed(1, 0)
    relayed(0, 1)
    z_tile(2, 2)
    z_tile(3, 2)
    relay(2, 1)
    relay(3, 1)
    relay(1, 2)
    expand((3, 0, 0))
    expand((1, 0, 0))
    relayed(2, 0)
    relayed(3, 0)
    relayed(1, 1)
    relayed(0, 2)
    relay(2, 2)
    relay(3, 2)
    expand((0, 0, 2))
    expand((0, 0, 3))
    expand((3, 0, 1))
    expand((1, 0, 1))
    expand((2, 0, 0))
    expand((3, 0, 2))
    expand((1, 0, 2))
    expand((3, 0, 3))
    expand((1, 0, 3))
    from_pair(0, 0)
    from_pair(0, 1)
    relayed(2, 1)
    relayed(3, 1)
    relayed(1, 2)
    from_pair(0, 2)
    from_pair(0, 3)
    from_pair(3, 0)
    from_pair(1, 0)
    from_pair(3, 1)
    from_pair(1, 1)
    expand((2, 0, 1))
    relayed(2, 2)
    relayed(3, 2)
    from_pair(2, 0)
    from_pair(2, 1)
    from_pair(3, 2)
    from_pair(1, 2)
    from_pair(3, 3)
    from_pair(1, 3)
    expand((2, 0, 2))
    expand((2, 0, 3))
    from_pair(2, 2)
    from_pair(2, 3)
    assert sent[0] == 93 * T
    remote(tri.at[pl.ds(0, 93)], tri.at[pl.ds(0, 93)], t_send, t_recv.at[0], pair).wait_send()
    remote(zrecv, zrecv, z_send, z_recv.at[0], pair).wait_send()
    for copy in started:
        copy.wait_send()

    norm = jnp.sqrt(jnp.sum(sq[...], keepdims=True))
    scale = 0.25 * (norm + DAMP * norm)
    inverse = 1.0 / scale
    damp = DAMP * norm * inverse
    root0 = lax.rsqrt(jnp.sqrt(scale))

    keep = 1.25 - 0.25 * damp
    take = 0.25 * inverse

    def product(rows, source):
        return jnp.dot(xb[source, rows, 0:BLK], full[0:BLK, :], preferred_element_type=F32)

    def affine(rows, source, target):
        new = keep * x[rows, :] - take * product(rows, source)
        x[rows, :] = new
        xb[target, rows, :] = new.astype(BF)

    def affines(rows, count):
        def step(s, carry):
            affine(rows, (s + 1) % 2, s % 2)
            return carry

        lax.fori_loop(0, count, step, 0)

    affine(G, 0, 1)
    t_ref[...] = x[G, :]
    affines(G, 4)
    p = 1.25 * t_ref[...] - 0.25 * damp * x[G, :] - take * product(G, 1)
    t_ref[...] = p
    total = jnp.sum(jnp.sum((p * p).reshape(XG // 8, 8, W), axis=0), keepdims=True) * (root0 * root0)

    def layer_start(n, buffer, peers):
        for k, to in enumerate(peers):
            remote(buffer.at[0], buffer.at[k + 1], r_send.at[n], r_recv.at[n], to).start()

    def layer_wait(n, buffer, count):
        others = buffer.at[pl.ds(1, count)]
        everything = remote(others, others, r_send.at[n], r_recv.at[n], pair)
        everything.wait_recv()
        everything.wait_send()

    red1[0] = jnp.broadcast_to(total, (1, T))
    layer_start(0, red1, [((dp + k) % n_dp, tensor) for k in range(1, n_dp)])
    row_ids = lax.broadcasted_iota(jnp.int32, (XR - XG, W), 0)
    col_ids = lax.broadcasted_iota(jnp.int32, (XR - XG, W), 1)
    unit = ((col_ids == row_ids + OWN * dp) & (row_ids < OWN)).astype(F32)
    xb[0, E, :] = unit.astype(BF)
    start = product(E, 0) * inverse + damp * unit
    x[E, :] = start
    xb[1, E, :] = start.astype(BF)
    affines(E, 2)
    layer_wait(0, red1, n_dp - 1)
    red2[0] = jnp.sum(red1[...], axis=0)
    layer_start(1, red2, [(dp, (tensor + k) % n_tensor) for k in range(1, n_tensor)])
    affines(E, 2)
    row_ids = lax.broadcasted_iota(jnp.int32, (OWN, BLK), 0)
    col_ids = lax.broadcasted_iota(jnp.int32, (OWN, BLK), 1)
    res_ref[...] = x[XG : XG + OWN, 0:BLK] - (col_ids == row_ids + OWN * dp).astype(F32)
    layer_wait(1, red2, n_tensor - 1)
    layer = jnp.sum(red2[...], axis=0)[:, 0:1]
    ratio = math.sqrt(D * FF) / jnp.sqrt(layer + EPSILON) * root0
    upd_ref[...] = (t_ref[0:ROWS, 0:BLK] * ratio).astype(BF)


def body(n_dp, n_tensor, gradient):
    dma = pltpu.SemaphoreType.DMA
    return pl.pallas_call(
        functools.partial(kernel, n_dp, n_tensor),
        out_shape=(
            jax.ShapeDtypeStruct((ROWS, BLK), BF),
            jax.ShapeDtypeStruct((OWN, BLK), F32),
        ),
        in_specs=[pl.BlockSpec(memory_space=pltpu.VMEM)],
        out_specs=(pl.BlockSpec(memory_space=pltpu.VMEM), pl.BlockSpec(memory_space=pltpu.VMEM)),
        scratch_shapes=[
            pltpu.VMEM((KD, EXT * T), BF),
            pltpu.VMEM((8 * KD, (NEED + 1) * T), BF),
            pltpu.VMEM((3, T, HALF * T), F32),
            pltpu.VMEM((CH, NZ - 1, T, T), BF),
            pltpu.VMEM((CH, NZ - 1, T, T), BF),
            pltpu.VMEM((96, T, T), BF),
            pltpu.VMEM((W, W), BF),
            pltpu.VMEM((XR, W), F32),
            pltpu.VMEM((2, XR, W), BF),
            pltpu.VMEM((XG, W), F32),
            pltpu.VMEM((8, T), F32),
            pltpu.VMEM((n_dp, 1, T), F32),
            pltpu.VMEM((n_tensor, 1, T), F32),
            dma((13,)),
            dma((13,)),
            dma,
            dma((CH,)),
            dma,
            dma((64,)),
            dma((2,)),
            dma((2,)),
        ],
        compiler_params=pltpu.CompilerParams(
            collective_id=0, has_side_effects=True, vmem_limit_bytes=48 * 1024 * 1024
        ),
        cost_estimate=pl.CostEstimate(flops=6_000_000_000, bytes_accessed=1_000_000, transcendentals=0),
    )(gradient)


def solution(mesh):
    return jax.shard_map(
        functools.partial(body, mesh.shape["dp"], mesh.shape["tensor"]),
        mesh=mesh,
        in_specs=(P("dp", "tensor"),),
        out_specs=(P("dp", "tensor"), P("dp", "tensor")),
        check_vma=False,
    )
```

```python
import functools
import math

import jax
import jax.numpy as jnp
from jax import lax
from jax.experimental import pallas as pl
from jax.experimental.pallas import tpu as pltpu
from jax.sharding import PartitionSpec as P

D = 3200
FF = 12800
BLK = 1600
DAMP = 0.002
EPSILON = 1e-06

T = 128
NB = 13
W = NB * T
HALF = 7
NEED = 10
EXT = 20
KD = 112
ROWS = 100
OWN = 50
XG = 104
XR = 160
NY, NZ, NC = 4, 4, 2
CH = 3
BF = jnp.bfloat16
F32 = jnp.float32
MESH = pl.DeviceIdType.MESH


def band_of(q):
    return q // HALF


def kernel(
    n_dp,
    n_tensor,
    g_ref,
    upd_ref,
    res_ref,
    gx,
    gall,
    acc,
    part,
    zrecv,
    tri,
    full,
    x,
    xb,
    t_ref,
    sq,
    red1,
    red2,
    g_send,
    g_recv,
    z_send,
    z_recv,
    t_send,
    t_recv,
    r_send,
    r_recv,
):
    dp = lax.axis_index("dp")
    tensor = lax.axis_index("tensor")
    a, b, c = dp // (NZ * NC), (dp // NC) % NZ, dp % NC

    def at(a_, b_, c_):
        return ((a_ * NZ + b_) * NC + c_, tensor)

    a_up, a_down = (a + 1) % NY, (a + NY - 1) % NY
    up = at(a_up, b, c)
    down = at(a_down, b, c)
    pair = at(a, b, 1 - c)
    zs = (b, b + 1 - 2 * (b % 2), (b + 2) % NZ, NZ - 1 - b)

    barrier = pltpu.get_barrier_semaphore()
    greeted = [(dp, (tensor + k) % n_tensor) for k in range(1, n_tensor)]
    greeted += [at(a, zs[k], c) for k in range(1, NZ)] + [up, down, pair]
    for to in greeted:
        pl.semaphore_signal(barrier, inc=1, device_id=to, device_id_type=MESH)

    def lanes(first, count):
        return pl.ds(pl.multiple_of(first * T, T), count * T)

    def rows(ra, rc):
        return pl.ds((2 * ra + rc) * KD, KD)

    tail = slice(ROWS - ROWS % 16, KD)
    gx[tail, :] = jnp.zeros((KD - tail.start, EXT * T), BF)
    gx[:, BLK - BLK % T : W] = jnp.zeros((KD, T), BF)
    gx[0:ROWS, 0:BLK] = g_ref[...]
    gx[0:ROWS, W:] = g_ref[:, 0 : EXT * T - W]

    first_band = [band_of(24 * v) for v in (a, a_up, a_down)]
    d_up = (first_band[1] + NB - first_band[0]) % NB
    d_down = (first_band[0] + NB - first_band[2]) % NB

    pl.semaphore_wait(barrier, len(greeted))

    def remote(src, dst, send, recv, to):
        return pltpu.make_async_remote_copy(
            src_ref=src, dst_ref=dst, send_sem=send, recv_sem=recv, device_id=to, device_id_type=MESH
        )

    started = []

    labels = [
        (3, 0, 3, 6),
        (1, 0, 1, 6),
        (3, 0, 0, 3),
        (3, 0, 9, 1),
        (1, 0, 0, 1),
        (1, 0, 7, 3),
        (2, 0, 0, 5),
        (2, 0, 5, 5),
        (0, 1, 0, NEED),
        (3, 1, 0, NEED),
        (1, 1, 0, NEED),
        (2, 1, 0, 5),
        (2, 1, 5, 5),
    ]

    def g_copy(n, src, to):
        ra, rc, first, count = labels[n]
        dst = gall.at[rows(ra, rc), pl.ds(first * T, count * T)]
        return remote(dst if src is None else src, dst, g_send.at[n], g_recv.at[n], to)

    def g_go(n, src, to):
        copy = g_copy(n, src, to)
        copy.start()
        started.append(copy)

    def g_own(n, base, to):
        g_go(n, gx.at[:, lanes(base + labels[n][2], labels[n][3])], to)

    def g_held(n, slot, first, to):
        g_go(n, gall.at[rows(*slot), lanes(first, labels[n][3])], to)

    def g_wait(n):
        g_copy(n, None, pair).wait_recv()

    q0 = 24 * a + 12 * c
    row0 = band_of(q0)
    local0 = row0 - first_band[0]

    def accumulate(start, count, first):
        for m in range(3):
            band = local0 + m
            value = lax.dot_general(
                gall[pl.ds(start, count), lanes(band, 1)],
                gall[pl.ds(start, count), lanes(band, HALF)],
                (((0,), (0,)), ((), ())),
                preferred_element_type=F32,
            )
            acc[m] = value if first else acc[m] + value

    g_own(0, first_band[1], up)
    g_own(1, first_band[2], down)
    g_own(8, first_band[0], pair)
    g_own(2, first_band[1], up)
    g_own(4, first_band[2], down)
    g_own(3, first_band[1], up)
    g_own(5, first_band[2], down)
    gall[0:KD, 0 : NEED * T] = gx[:, lanes(first_band[0], NEED)]
    gall[:, NEED * T :] = jnp.zeros((8 * KD, T), BF)
    sq[...] = jnp.zeros_like(sq)
    G, E = pl.ds(0, XG), pl.ds(XG, XR - XG)
    xb[0, G, :] = gx[0:XG, 0:W]
    x[G, :] = gx[0:XG, 0:W].astype(F32)
    g_wait(8)
    accumulate(0, 2 * KD, True)
    g_wait(0)
    g_held(6, (3, 0), d_up, up)
    g_wait(1)
    g_held(7, (1, 0), 5 - d_down, down)
    g_wait(2)
    g_wait(3)
    g_held(9, (3, 0), 0, pair)
    g_wait(4)
    g_wait(5)
    g_held(10, (1, 0), 0, pair)
    g_wait(9)
    accumulate(6 * KD, 2 * KD, False)
    g_wait(10)
    accumulate(2 * KD, 2 * KD, False)
    g_wait(6)
    g_held(11, (2, 0), 0, pair)
    g_wait(7)
    g_held(12, (2, 0), 5, pair)
    accumulate(4 * KD, KD, False)
    g_wait(11)
    g_wait(12)
    accumulate(5 * KD, KD, False)

    def held_tile(e):
        q = q0 + e
        return acc[band_of(q) - row0, :, lanes(q % HALF, 1)]

    def place(label, e):
        ra, rc, k = label
        return 24 * ((a + ra) % NY) + 12 * (c if rc == 0 else 1 - c) + CH * zs[k] + e

    def slot(label, e):
        ra, rc, k = label
        return 48 + ra * NZ + k if rc else (ra * NZ + k) * CH + e

    ALL, LO, HI = pl.ds(0, T), pl.ds(0, T // 2), pl.ds(T // 2, T // 2)
    sent = [0]

    def t_go(held, label, e, to, piece=ALL):
        tile = tri.at[place(held, e), piece, :]
        remote(tile, tile, t_send, t_recv.at[slot(label, e)], to).start()
        sent[0] += piece.size

    def t_wait(label, e):
        tiles = tri.at[place(label, e)] if label[1] == 0 else tri.at[pl.ds(place(label, 0), CH)]
        remote(tiles, tiles, t_send, t_recv.at[slot(label, e)], pair).wait_recv()

    def expand(label):
        first = place(label, 0)

        def tile(e, carry):
            q = first + e

            @pl.when(q < NB * HALF)
            def _():
                i = band_of(q)
                j = (i + q % HALF) % NB
                value = tri[q]
                wide = value.astype(F32)
                weight = jnp.where(q % HALF == 0, 1.0, 2.0)
                sq[...] += weight * jnp.sum((wide * wide).reshape(T // 8, 8, T), axis=0)
                full[lanes(j, 1), lanes(i, 1)] = value.T
                full[lanes(i, 1), lanes(j, 1)] = value

            return carry

        lax.fori_loop(0, CH, tile, 0)

    def z_sum(e):
        remote(zrecv.at[e], zrecv.at[e], z_send, z_recv.at[e], pair).wait_recv()
        total = held_tile(CH * b + e)
        for k in range(NZ - 1):
            total = total + zrecv[e, k].astype(F32)
        tri[place((0, 0, 0), e)] = total.astype(BF)
        for k in range(1, NZ):
            t_go((0, 0, 0), (0, 0, k), e, at(a, zs[k], c))
        spread(0, e)

    def spread(k, e):
        t_go((0, 0, k), (3, 0, k), e, up)
        t_go((0, 0, k), (1, 0, k), e, down)
        t_go((0, 0, k), (0, 1, k), e, pair)

    def z_tile(k, e):
        t_wait((0, 0, k), e)
        spread(k, e)

    def relay(k, e):
        t_wait((3, 0, k), e)
        t_go((3, 0, k), (2, 0, k), e, up, LO)
        t_wait((1, 0, k), e)
        t_go((1, 0, k), (2, 0, k), e, down, HI)
        t_go((3, 0, k), (3, 1, k), e, pair)
        t_go((1, 0, k), (1, 1, k), e, pair)

    def relayed(k, e):
        t_wait((2, 0, k), e)
        t_go((2, 0, k), (2, 1, k), e, pair)

    def from_pair(ra, k):
        t_wait((ra, 1, k), 0)
        expand((ra, 1, k))

    for e in range(CH):
        for k in (2, 3, 1):
            part[e, k - 1] = held_tile(CH * zs[k] + e).astype(BF)
            remote(
                part.at[e, k - 1], zrecv.at[e, k - 1], z_send, z_recv.at[e], at(a, zs[k], c)
            ).start()
    z_sum(0)
    z_tile(1, 0)
    z_sum(1)
    relay(0, 0)
    z_tile(1, 1)
    z_tile(2, 0)
    z_tile(3, 0)
    z_sum(2)
    relay(1, 0)
    relay(0, 1)
    relayed(0, 0)
    z_tile(2, 1)
    z_tile(3, 1)
    relay(2, 0)
    relay(3, 0)
    relay(1, 1)
    z_tile(1, 2)
    relay(0, 2)
    expand((0, 0, 0))
    expand((0, 0, 1))
    relayed(1, 0)
    relayed(0, 1)
    z_tile(2, 2)
    z_tile(3, 2)
    relay(2, 1)
    relay(3, 1)
    relay(1, 2)
    expand((3, 0, 0))
    expand((1, 0, 0))
    relayed(2, 0)
    relayed(3, 0)
    relayed(1, 1)
    relayed(0, 2)
    relay(2, 2)
    relay(3, 2)
    expand((0, 0, 2))
    expand((0, 0, 3))
    expand((3, 0, 1))
    expand((1, 0, 1))
    expand((2, 0, 0))
    expand((3, 0, 2))
    expand((1, 0, 2))
    expand((3, 0, 3))
    expand((1, 0, 3))
    from_pair(0, 0)
    from_pair(0, 1)
    relayed(2, 1)
    relayed(3, 1)
    relayed(1, 2)
    from_pair(0, 2)
    from_pair(0, 3)
    from_pair(3, 0)
    from_pair(1, 0)
    from_pair(3, 1)
    from_pair(1, 1)
    expand((2, 0, 1))
    relayed(2, 2)
    relayed(3, 2)
    from_pair(2, 0)
    from_pair(2, 1)
    from_pair(3, 2)
    from_pair(1, 2)
    from_pair(3, 3)
    from_pair(1, 3)
    expand((2, 0, 2))
    expand((2, 0, 3))
    from_pair(2, 2)
    from_pair(2, 3)
    assert sent[0] == 93 * T
    remote(tri.at[pl.ds(0, 93)], tri.at[pl.ds(0, 93)], t_send, t_recv.at[0], pair).wait_send()
    remote(zrecv, zrecv, z_send, z_recv.at[0], pair).wait_send()
    for copy in started:
        copy.wait_send()

    norm = jnp.sqrt(jnp.sum(sq[...], keepdims=True))
    scale = 0.25 * (norm + DAMP * norm)
    inverse = 1.0 / scale
    damp = DAMP * norm * inverse
    root0 = lax.rsqrt(jnp.sqrt(scale))

    keep = 1.25 - 0.25 * damp
    take = 0.25 * inverse

    def product(rows, source):
        return jnp.dot(xb[source, rows, 0:BLK], full[0:BLK, :], preferred_element_type=F32)

    def affine(rows, source, target):
        new = keep * x[rows, :] - take * product(rows, source)
        x[rows, :] = new
        xb[target, rows, :] = new.astype(BF)

    def affines(rows, count):
        def step(s, carry):
            affine(rows, (s + 1) % 2, s % 2)
            return carry

        lax.fori_loop(0, count, step, 0)

    affine(G, 0, 1)
    t_ref[...] = x[G, :]
    affines(G, 4)
    p = 1.25 * t_ref[...] - 0.25 * damp * x[G, :] - take * product(G, 1)
    t_ref[...] = p
    total = jnp.sum(jnp.sum((p * p).reshape(XG // 8, 8, W), axis=0), keepdims=True) * (root0 * root0)

    def layer_start(n, buffer, peers):
        for k, to in enumerate(peers):
            remote(buffer.at[0], buffer.at[k + 1], r_send.at[n], r_recv.at[n], to).start()

    def layer_wait(n, buffer, count):
        others = buffer.at[pl.ds(1, count)]
        everything = remote(others, others, r_send.at[n], r_recv.at[n], pair)
        everything.wait_recv()
        everything.wait_send()

    red1[0] = jnp.broadcast_to(total, (1, T))
    layer_start(0, red1, [((dp + k) % n_dp, tensor) for k in range(1, n_dp)])
    row_ids = lax.broadcasted_iota(jnp.int32, (XR - XG, W), 0)
    col_ids = lax.broadcasted_iota(jnp.int32, (XR - XG, W), 1)
    unit = ((col_ids == row_ids + OWN * dp) & (row_ids < OWN)).astype(F32)
    xb[0, E, :] = unit.astype(BF)
    start = product(E, 0) * inverse + damp * unit
    x[E, :] = start
    xb[1, E, :] = start.astype(BF)
    affines(E, 2)
    layer_wait(0, red1, n_dp - 1)
    red2[0] = jnp.sum(red1[...], axis=0)
    layer_start(1, red2, [(dp, (tensor + k) % n_tensor) for k in range(1, n_tensor)])
    affines(E, 2)
    row_ids = lax.broadcasted_iota(jnp.int32, (OWN, BLK), 0)
    col_ids = lax.broadcasted_iota(jnp.int32, (OWN, BLK), 1)
    res_ref[...] = x[XG : XG + OWN, 0:BLK] - (col_ids == row_ids + OWN * dp).astype(F32)
    layer_wait(1, red2, n_tensor - 1)
    layer = jnp.sum(red2[...], axis=0)[:, 0:1]
    ratio = math.sqrt(D * FF) / jnp.sqrt(layer + EPSILON) * root0
    upd_ref[...] = (t_ref[0:ROWS, 0:BLK] * ratio).astype(BF)


def body(n_dp, n_tensor, gradient):
    dma = pltpu.SemaphoreType.DMA
    return pl.pallas_call(
        functools.partial(kernel, n_dp, n_tensor),
        out_shape=(
            jax.ShapeDtypeStruct((ROWS, BLK), BF),
            jax.ShapeDtypeStruct((OWN, BLK), F32),
        ),
        in_specs=[pl.BlockSpec(memory_space=pltpu.VMEM)],
        out_specs=(pl.BlockSpec(memory_space=pltpu.VMEM), pl.BlockSpec(memory_space=pltpu.VMEM)),
        scratch_shapes=[
            pltpu.VMEM((KD, EXT * T), BF),
            pltpu.VMEM((8 * KD, (NEED + 1) * T), BF),
            pltpu.VMEM((3, T, HALF * T), F32),
            pltpu.VMEM((CH, NZ - 1, T, T), BF),
            pltpu.VMEM((CH, NZ - 1, T, T), BF),
            pltpu.VMEM((96, T, T), BF),
            pltpu.VMEM((W, W), BF),
            pltpu.VMEM((XR, W), F32),
            pltpu.VMEM((2, XR, W), BF),
            pltpu.VMEM((XG, W), F32),
            pltpu.VMEM((8, T), F32),
            pltpu.VMEM((n_dp, 1, T), F32),
            pltpu.VMEM((n_tensor, 1, T), F32),
            dma((13,)),
            dma((13,)),
            dma,
            dma((CH,)),
            dma,
            dma((64,)),
            dma((2,)),
            dma((2,)),
        ],
        compiler_params=pltpu.CompilerParams(
            collective_id=0, has_side_effects=True, vmem_limit_bytes=48 * 1024 * 1024
        ),
        cost_estimate=pl.CostEstimate(flops=6_000_000_000, bytes_accessed=1_000_000, transcendentals=0),
    )(gradient)


def solution(mesh):
    return jax.shard_map(
        functools.partial(body, mesh.shape["dp"], mesh.shape["tensor"]),
        mesh=mesh,
        in_specs=(P("dp", "tensor"),),
        out_specs=(P("dp", "tensor"), P("dp", "tensor")),
        check_vma=False,
    )
```
